512 devices in a mesh: dp: 64 (over x, z), mp: 8 (over y, core).
Axes of the slice: x: 4, y: 4, z: 16, core: 2. Of those that a mesh axis runs over, the one named last changes fastest.
Arguments:
- resp_q: bfloat16 [64, 128, 8192], P('dp', None, 'mp'), may hold values from -12 to 12, as said below
- resp_kv: bfloat16 [2, 64, 128, 1024], P(None, 'dp', None, 'mp'), may hold values from -4 to 4
- d_out: bfloat16 [64, 128, 8192], P('dp', None, 'mp'), may hold values from -6 to 6
- lengths: int32 [64], P('dp'), may hold values from 1 to 128, 6144 in all
- fork: int32 [64], replicated, may hold values from 0 to 127
- page_table: int32 [128, 32], replicated, may hold values from 0 to 4095, as said below
- pool_pages: bfloat16 [4096, 2, 16, 1024], P(('dp', 'mp')), may hold values from -4 to 4
- pool_scales: bfloat16 [4096, 2, 8], P(('dp', 'mp')), may hold values from 0.29882812 to 3
Outputs:
- d_query: bfloat16 [64, 128, 8192], P('dp', None, 'mp')
- d_resp_kv: bfloat16 [2, 64, 128, 1024], P(None, 'dp', None, 'mp')
- d_pool: float32 [4096, 2, 16, 1024], P(('dp', 'mp'))
The draws below stay inside these ranges and needn't reach their ends.
Inputs may be any that keep to these rules, and one draw needn't show every extreme that they name: `page_table`: every pool page is named exactly once. Pool page g lies on dp index g // 64, and the 32 pages of one prompt lie on 32 different dp indices. `resp_q`: query entries. On some rows, some query heads may be a multiple between 1.5 and 3 of a key of the same response, so that scores can reach several hundred.
All inputs are finite; a program needn't handle non-finite values. No bound on the sum of `lengths` on one device may be relied on, other than what follows from the above.
Results may differ from the reference program's by a relative error of at most 0.012.
Values may be sent and summed in bfloat16 or wider, within the bound.
No kernel may reach another device: no remote copies, remote signals or barrier semaphores. Data moves between devices by JAX's collectives and lax.ppermute only.
A program may use at most 64 MiB of HBM per device.

```python
import math
import jax
import jax.numpy as jnp
import numpy as np
from jax import lax

HQ = 64
KVH = 8
DH = 128
GROUP = 8
PAGE = 16
RLEN = 128
PAGES_DEV = 8
PAGES = 32
RESPONSES = 64
PROMPTS = 128
POOL = 4096
N_DP = 64
N_MP = 8


def shared_keys(key, strength):
    base_keys = jnp.clip(jax.random.normal(key, (RESPONSES, RLEN, KVH * DH), jnp.float32), -4.0, 4.0)
    step_pos = jnp.arange(RLEN)
    marked = (step_pos % 29 == 7).astype(jnp.float32)[None, :, None] * strength
    following = jnp.roll(marked, -1, axis=1)
    signs = jnp.where(base_keys >= 0.0, 1.0, -1.0)
    big_keys = 4.0 * signs
    lowered = (jnp.arange(KVH * DH) % DH < max(DH // 16, 1)).astype(jnp.float32)[None, None, :]
    near_keys = big_keys * (1.0 - lowered) + 3.75 * signs * lowered
    following_near = jnp.roll(near_keys, -1, axis=1)
    mixed_keys = base_keys * (1.0 - marked - following) + following * following_near
    return (mixed_keys, marked)


def draw_resp_q(key, part):
    strength = 0.0
    mixed_keys, marked = shared_keys(key, strength)
    key = jax.random.fold_in(key, 3)
    drawn_rows = jnp.clip(jax.random.normal(key, (RESPONSES, RLEN, KVH, HQ // KVH, DH), jnp.float32), -4.0, 4.0)
    head_ids = jnp.arange(HQ).reshape(KVH, HQ // KVH)
    head_mark = (head_ids % 4 == 1).astype(jnp.float32)[None, None, :, :, None]
    chosen = marked[..., None, None] * head_mark
    result = drawn_rows * (1.0 - chosen)
    return result.reshape(RESPONSES, RLEN, HQ * DH).astype(jnp.bfloat16)


def draw_resp_kv(key, part):
    strength = 0.0
    mixed_keys, marked = shared_keys(key, strength)
    key = jax.random.fold_in(key, 5)
    values = jnp.clip(jax.random.normal(key, (RESPONSES, RLEN, KVH * DH), jnp.float32), -4.0, 4.0)
    return jnp.stack([mixed_keys, values]).astype(jnp.bfloat16)


def draw_page_table(key, part):
    key = jax.random.fold_in(key, 7)
    key_spread, key_shift, key_slot, key_order = jax.random.split(key, 4)
    per_dev = N_MP * PAGES_DEV
    spread = jax.random.permutation(key_spread, N_DP)
    shifts = jax.random.randint(key_shift, (per_dev,), 0, N_DP)
    scores = jax.random.randint(key_slot, (N_DP, per_dev), 0, 1 << 20) * per_dev + jnp.arange(per_dev)[None, :]
    slot_of = jnp.argsort(scores, axis=1)
    prompt_order = jax.random.permutation(key_order, PROMPTS)
    half_index = prompt_order // per_dev
    column = prompt_order % per_dev
    logical = jnp.arange(PAGES)
    position = (half_index[:, None] * PAGES + logical[None, :] + shifts[column][:, None]) % N_DP
    device = spread[position]
    slot_index = slot_of[device, column[:, None]]
    return (device * per_dev + slot_index).astype(jnp.int32)


def touch_ends(values, stream_key, low, top_value):
    dims = values.shape
    spot = [jax.random.randint(jax.random.fold_in(stream_key, axis), (), 0, dims[axis]) for axis in range(len(dims))]
    values = values.at[tuple(spot)].set(low)
    longest = dims.index(max(dims))
    spot[longest] = (spot[longest] + 1) % dims[longest]
    return values.at[tuple(spot)].set(top_value)


def level_of(own_key, shape, cuts, least, top_value):
    def one(dim, parts):
        heights = jax.random.uniform(jax.random.fold_in(jax.random.fold_in(own_key, 6), dim), (parts,), jnp.float32, least / len(cuts), top_value / len(cuts))
        return jnp.repeat(jnp.exp(heights), shape[dim] // parts).reshape((-1,) + (1,) * (len(shape) - dim - 1))

    level = one(*cuts[0])
    for cut in cuts[1:]:
        level = level * one(*cut)
    return level


def cumulative_ranks(number_of, slope):
    loads = [(1 << 20) // math.isqrt(grade ** slope) + 1 for grade in range(1, number_of + 1)]
    deviation = 1 + sum(loads) // (1 << 30)
    return np.cumsum(np.array([max(1, weight // deviation) for weight in loads]))


def skewed_ids(own_key, extent, number_of, lean):
    listing = cumulative_ranks(number_of, lean)
    ticket = jax.random.randint(jax.random.fold_in(own_key, 1), extent, 0, int(listing[number_of - 1]))
    rank = jnp.searchsorted(jnp.asarray(listing, jnp.int32), ticket, side="right")
    return jax.random.permutation(jax.random.fold_in(own_key, 2), number_of)[rank].astype(jnp.int32)


def length_profile(amount, total, limit, slope):
    loads = [(1 << 20) // math.isqrt(standing ** slope) + 1 for standing in range(2, amount + 1)]
    spare, holding = total - limit - (amount - 1), [1] * (amount - 1)
    while spare > 0:
        movable = [i for i in range(amount - 1) if holding[i] < limit]
        mass, budget = sum([loads[i] for i in movable]), spare
        for i in movable:
            addition = min(limit - holding[i], max(1, budget * loads[i] // mass), spare)
            holding[i] = holding[i] + addition
            spare = spare - addition
    return np.array([limit] + holding)


def uneven(own_key, count, total, limit, skew):
    if count == 2:
        one = jax.random.randint(own_key, (), max(1, total - limit), min(limit, total - 1) + 1)
        return jnp.stack([one, total - one])
    tallies = jnp.asarray(length_profile(count, total, limit, skew), jnp.int32)
    couples = (count - 1) // 2
    donor, taker = tallies[1:1 + 2 * couples:2], tallies[2:2 + 2 * couples:2]
    slack = jnp.minimum(donor - 1, limit - taker)
    moved = jax.random.randint(jax.random.fold_in(own_key, 1), (couples,), 0, 1 << 20) % (slack + 1)
    tallies = tallies.at[1:1 + 2 * couples:2].set(donor - moved).at[2:2 + 2 * couples:2].set(taker + moved)
    return tallies[jax.random.permutation(jax.random.fold_in(own_key, 2), count)]


def normal_values(key, dims, scale, limit, pieces=(), kind=jnp.bfloat16):
    values = jax.random.normal(key, dims, jnp.float32) * scale
    if len(pieces) > 0:
        values = level_of(key, dims, pieces, -0.22, 0.18) * values
    return jnp.clip(values, min=-limit, max=limit).astype(kind)


def setup_inputs(seed: int = 0) -> dict:
    arg_keys = jax.random.split(jax.random.key(seed), 9)
    resp_q = draw_resp_q(jax.random.fold_in(arg_keys[8], 71), 0)
    resp_kv = draw_resp_kv(jax.random.fold_in(arg_keys[8], 71), 0)
    d_out = normal_values(arg_keys[2], (RESPONSES, RLEN, HQ * DH), 1.0, 6.0, ((0, 64), (2, 8)))
    lengths = uneven(arg_keys[3], RESPONSES, RESPONSES * RLEN * 3 // 4, RLEN, 1).astype(jnp.int32)
    fork = touch_ends(skewed_ids(arg_keys[4], (RESPONSES,), PROMPTS, 2), jax.random.fold_in(arg_keys[4], 3), 0, PROMPTS - 1).astype(jnp.int32)
    page_table = draw_page_table(jax.random.fold_in(arg_keys[8], 71), 0)
    pool_pages = normal_values(arg_keys[6], (POOL, 2, PAGE, KVH * DH), 1.0, 4.0, ((0, 512),))
    pool_scales = jnp.clip(jnp.exp(math.log(3.0) - 2.306499 * jax.random.uniform(arg_keys[7], (POOL, 2, KVH), jnp.float32) ** level_of(arg_keys[7], (POOL, 2, KVH), ((0, 512),), -0.2, 0.2)), 0.29882812, 3.0).astype(jnp.bfloat16)
    return {"resp_q": resp_q, "resp_kv": resp_kv, "d_out": d_out, "lengths": lengths, "fork": fork, "page_table": page_table, "pool_pages": pool_pages, "pool_scales": pool_scales}


def dequantize(stored, factors):
    heads = factors.shape[-1]
    head_width = stored.shape[-1] // heads
    shaped = stored.astype(jnp.float32).reshape(stored.shape[0], 2, stored.shape[2], heads, head_width)
    scaled = shaped * factors.astype(jnp.float32).reshape(stored.shape[0], 2, 1, heads, 1)
    return scaled.astype(jnp.bfloat16).reshape(stored.shape)


def one_response(query_rows, own_kv, grad_rows, length, prompt_pages):
    prompt_len = PAGES * PAGE
    total = prompt_len + RLEN
    inv_root = 1.0 / (DH ** 0.5)
    key_all = jnp.concatenate([prompt_pages[:, 0].reshape(prompt_len, KVH * DH), own_kv[0]], 0)
    value_all = jnp.concatenate([prompt_pages[:, 1].reshape(prompt_len, KVH * DH), own_kv[1]], 0)
    key_heads = key_all.reshape(total, KVH, DH).transpose(1, 0, 2).astype(jnp.float32)
    value_heads = value_all.reshape(total, KVH, DH).transpose(1, 0, 2).astype(jnp.float32)
    row_pos = jnp.arange(RLEN)
    live = (row_pos < length)[:, None]
    grad_masked = jnp.where(live, grad_rows, jnp.zeros_like(grad_rows))
    query_heads = query_rows.reshape(RLEN, KVH, GROUP, DH).transpose(1, 2, 0, 3).astype(jnp.float32)
    grad_heads = grad_masked.reshape(RLEN, KVH, GROUP, DH).transpose(1, 2, 0, 3).astype(jnp.float32)
    scores = jnp.einsum("jgtd,jud->jgtu", query_heads, key_heads) * inv_root
    key_cols = jnp.arange(total)
    allowed = (key_cols[None, :] < prompt_len) | (key_cols[None, :] - prompt_len <= row_pos[:, None])
    scores = jnp.where(allowed, scores, -1e30)
    row_max = jnp.max(scores, axis=-1, keepdims=True)
    exp_scores = jnp.exp(scores - row_max)
    weights = exp_scores / jnp.sum(exp_scores, axis=-1, keepdims=True)
    weights_b = lax.optimization_barrier(weights.astype(jnp.bfloat16)).astype(jnp.float32)
    attn_out = jnp.einsum("jgtu,jud->jgtd", weights_b, value_heads)
    row_delta = jnp.sum(grad_heads * attn_out, axis=-1)
    grad_weights = jnp.einsum("jgtd,jud->jgtu", grad_heads, value_heads)
    grad_scores = weights * (grad_weights - row_delta[..., None])
    grad_scores = lax.optimization_barrier(grad_scores.astype(jnp.bfloat16)).astype(jnp.float32)
    grad_query = jnp.einsum("jgtu,jud->jgtd", grad_scores, key_heads) * inv_root
    grad_query = grad_query.transpose(2, 0, 1, 3).reshape(RLEN, HQ * DH).astype(jnp.bfloat16)
    grad_keys = jnp.einsum("jgtu,jgtd->jud", grad_scores, query_heads) * inv_root
    grad_values = jnp.einsum("jgtu,jgtd->jud", weights_b, grad_heads)
    own_keys = grad_keys[:, prompt_len:].transpose(1, 0, 2).reshape(RLEN, KVH * DH)
    own_values = grad_values[:, prompt_len:].transpose(1, 0, 2).reshape(RLEN, KVH * DH)
    own_grads = jnp.stack([own_keys, own_values]).astype(jnp.bfloat16)
    prompt_grad = jnp.stack([grad_keys[:, :prompt_len], grad_values[:, :prompt_len]])
    prompt_grad = prompt_grad.reshape(2, KVH, PAGES, PAGE, DH).transpose(2, 0, 3, 1, 4).reshape(PAGES, 2, PAGE, KVH * DH)
    return grad_query, own_grads, prompt_grad


def reference(resp_q, resp_kv, d_out, lengths, fork, page_table, pool_pages, pool_scales):
    def step_fn(pool_grad, block_items):
        query_rows, own_kv, grad_rows, length, prompt = block_items
        page_ids = page_table[prompt]
        prompt_pages = dequantize(pool_pages[page_ids], pool_scales[page_ids])
        grad_query, own_grads, prompt_grad = one_response(query_rows, own_kv, grad_rows, length, prompt_pages)
        pool_grad = pool_grad.at[page_ids].add(prompt_grad)
        return pool_grad, (grad_query, own_grads)

    start = jnp.zeros(pool_pages.shape, jnp.float32)
    pool_grad, (d_query, own_all) = lax.scan(step_fn, start, (resp_q, resp_kv.transpose(1, 0, 2, 3), d_out, lengths, fork))
    return d_query, own_all.transpose(1, 0, 2, 3), pool_grad
```

```python
import functools
import math

import jax
import jax.numpy as jnp
from jax import lax
from jax.experimental import pallas as pl
from jax.experimental.pallas import tpu as pltpu
from jax.sharding import PartitionSpec as P

DH = 128
SMEM = pl.BlockSpec(memory_space=pltpu.SMEM)
VMEM = pl.BlockSpec(memory_space=pltpu.VMEM)
PARAMS = pltpu.CompilerParams(vmem_limit_bytes=48 * 1024 * 1024)


def scale_kernel(pages_ref, scales_ref, out_ref):
    rows = pages_ref.shape[0]
    heads = scales_ref.shape[1]
    factors = scales_ref[...].astype(jnp.float32)
    repeat = rows // factors.shape[0]
    factors = jnp.broadcast_to(factors[:, None, :], (factors.shape[0], repeat, heads))
    factors = factors.reshape(rows, heads)
    for j in range(heads):
        stored = pages_ref[:, j * DH : (j + 1) * DH].astype(jnp.float32)
        out_ref[j] = (stored * factors[:, j : j + 1]).astype(jnp.bfloat16)


def select_kernel(rows_ref, pages_ref, out_ref):
    for r in range(out_ref.shape[0]):
        out_ref[r] = pages_ref[rows_ref[r]]


def attention_kernel(
    page_rows,
    sources_ref,
    length_ref,
    arrived_ref,
    own_ref,
    q_ref,
    g_ref,
    d_query_ref,
    d_own_ref,
    sent_ref,
    key_ref,
    value_ref,
):
    pages = sources_ref.shape[0]
    prompt_len = pages * page_rows
    resp_len = q_ref.shape[0]
    heads = q_ref.shape[1] // DH
    per_block = 2
    width = per_block * resp_len
    inv_root = 1.0 / DH**0.5
    to_exp2 = inv_root * math.log2(math.e)
    for i in range(pages):
        slot = sources_ref[i]
        key_ref[i * page_rows : (i + 1) * page_rows] = arrived_ref[slot, :page_rows]
        value_ref[i * page_rows : (i + 1) * page_rows] = arrived_ref[slot, page_rows:]
    key_ref[prompt_len:] = own_ref[0]
    value_ref[prompt_len:] = own_ref[1]
    keys = key_ref[...]
    values = value_ref[...]
    keys_t = keys.astype(jnp.float32).T.astype(jnp.bfloat16)
    live = lax.broadcasted_iota(jnp.int32, (resp_len, DH), 0) < length_ref[0]
    across = (((1,), (1,)), ((), ()))
    own_pos = lax.broadcasted_iota(jnp.int32, (resp_len, width), 0)
    row_pos = lax.broadcasted_iota(jnp.int32, (resp_len, width), 1) % resp_len
    allowed = own_pos <= row_pos
    key_grad = None
    value_grad = None
    for b in range(heads // per_block):
        cols = [slice((b * per_block + k) * DH, (b * per_block + k + 1) * DH) for k in range(per_block)]
        q = jnp.concatenate([q_ref[:, c] for c in cols], axis=0)
        g = jnp.concatenate([jnp.where(live, g_ref[:, c], jnp.zeros_like(g_ref[:, c])) for c in cols], axis=0)
        scores = lax.dot_general(keys, q, across, preferred_element_type=jnp.float32) * to_exp2
        prompt_scores = scores[:prompt_len]
        own_scores = jnp.where(allowed, scores[prompt_len:], -1e30)
        top = jnp.maximum(
            jnp.max(prompt_scores, axis=0, keepdims=True), jnp.max(own_scores, axis=0, keepdims=True)
        )
        exps = jnp.exp2(jnp.concatenate([prompt_scores, own_scores], axis=0) - top)
        weights = exps * (1.0 / jnp.sum(exps, axis=0, keepdims=True))
        weights_b = weights.astype(jnp.bfloat16)
        grad_weights = lax.dot_general(values, g, across, preferred_element_type=jnp.float32)
        delta = jnp.sum(weights_b.astype(jnp.float32) * grad_weights, axis=0, keepdims=True)
        grad_scores = (weights * (grad_weights - delta)).astype(jnp.bfloat16)
        part = jnp.dot(weights_b, g, preferred_element_type=jnp.float32)
        value_grad = part if value_grad is None else value_grad + part
        part = jnp.dot(grad_scores, q, preferred_element_type=jnp.float32)
        key_grad = part if key_grad is None else key_grad + part
        d_q = jnp.dot(keys_t, grad_scores, preferred_element_type=jnp.float32) * inv_root
        for k, c in enumerate(cols):
            d_query_ref[:, c] = d_q[:, k * resp_len : (k + 1) * resp_len].T.astype(jnp.bfloat16)
    key_grad = (key_grad * inv_root).astype(jnp.bfloat16)
    value_grad = value_grad.astype(jnp.bfloat16)
    d_own_ref[0] = key_grad[prompt_len:]
    d_own_ref[1] = value_grad[prompt_len:]
    for i in range(pages):
        slot = sources_ref[i]
        sent_ref[slot, :page_rows] = key_grad[i * page_rows : (i + 1) * page_rows]
        sent_ref[slot, page_rows:] = value_grad[i * page_rows : (i + 1) * page_rows]


def sum_kernel(rows_ref, arrived_ref, out_ref, total_ref):
    pages = out_ref.shape[0]
    total_ref[...] = jnp.zeros_like(total_ref)
    for r in range(arrived_ref.shape[0]):
        row = rows_ref[r]
        total_ref[row] = total_ref[row] + arrived_ref[r].astype(jnp.float32)
    out_ref[...] = total_ref[:pages].astype(jnp.bfloat16)


def layout_kernel(parts_ref, out_ref):
    for j in range(parts_ref.shape[0]):
        out_ref[:, j * DH : (j + 1) * DH] = parts_ref[j].astype(jnp.float32)


def per_device(resp_q, resp_kv, d_out, lengths, fork, page_table, pool_pages, pool_scales):
    dp_size = lax.axis_size("dp")
    mp_size = lax.axis_size("mp")
    my_dp = lax.axis_index("dp")
    pool_dev, _, page_rows, _ = pool_pages.shape
    heads_kv = pool_scales.shape[-1]
    pages_prompt = page_table.shape[1]
    resp_len = resp_q.shape[1]
    total = pages_prompt * page_rows + resp_len
    group_rows = mp_size * pool_dev
    slot_rows = 2 * page_rows
    bf16 = jnp.bfloat16

    by_head = pl.pallas_call(
        scale_kernel,
        out_shape=jax.ShapeDtypeStruct((heads_kv, pool_dev * slot_rows, DH), bf16),
        in_specs=[VMEM, VMEM],
        out_specs=VMEM,
        compiler_params=PARAMS,
    )(pool_pages.reshape(pool_dev * slot_rows, -1), pool_scales.reshape(pool_dev * 2, heads_kv))
    regrouped = lax.all_to_all(by_head, "mp", split_axis=0, concat_axis=0, tiled=True)
    regrouped = regrouped.reshape(group_rows, slot_rows, DH)

    wanted = jnp.take(page_table, fork, axis=0)
    on_device = wanted // group_rows == my_dp
    send_rows = jnp.sum(jnp.where(on_device, wanted % group_rows, 0), axis=1)
    sum_rows = jnp.where(jnp.any(on_device, axis=1), send_rows, group_rows)
    sources = jnp.take(wanted, my_dp, axis=0) // group_rows

    slots = jax.ShapeDtypeStruct((dp_size, slot_rows, DH), bf16)
    selected = pl.pallas_call(
        select_kernel,
        out_shape=slots,
        in_specs=[SMEM, VMEM],
        out_specs=VMEM,
        compiler_params=PARAMS,
    )(send_rows, regrouped)
    arrived = lax.all_to_all(selected, "dp", split_axis=0, concat_axis=0, tiled=True)

    d_query, d_own, sent = pl.pallas_call(
        functools.partial(attention_kernel, page_rows),
        out_shape=(
            jax.ShapeDtypeStruct(resp_q.shape[1:], bf16),
            jax.ShapeDtypeStruct((2, resp_len, DH), bf16),
            slots,
        ),
        in_specs=[SMEM, SMEM, VMEM, VMEM, VMEM, VMEM],
        out_specs=(VMEM, VMEM, VMEM),
        scratch_shapes=[pltpu.VMEM((total, DH), bf16), pltpu.VMEM((total, DH), bf16)],
        compiler_params=PARAMS,
    )(sources, lengths, arrived, resp_kv[:, 0], resp_q[0], d_out[0])

    returned = lax.all_to_all(sent, "dp", split_axis=0, concat_axis=0, tiled=True)
    summed = pl.pallas_call(
        sum_kernel,
        out_shape=jax.ShapeDtypeStruct((group_rows, slot_rows, DH), bf16),
        in_specs=[SMEM, VMEM],
        out_specs=VMEM,
        scratch_shapes=[pltpu.VMEM((group_rows + 1, slot_rows, DH), jnp.float32)],
        compiler_params=PARAMS,
    )(sum_rows, returned)
    restored = lax.all_to_all(
        summed.reshape(mp_size, pool_dev * slot_rows, DH), "mp", split_axis=0, concat_axis=0, tiled=True
    )
    d_pool = pl.pallas_call(
        layout_kernel,
        out_shape=jax.ShapeDtypeStruct((pool_dev * slot_rows, heads_kv * DH), jnp.float32),
        in_specs=[VMEM],
        out_specs=VMEM,
        compiler_params=PARAMS,
    )(restored)
    return d_query[None], d_own[:, None], d_pool.reshape(pool_pages.shape)


def solution(mesh):
    return jax.shard_map(
        per_device,
        mesh=mesh,
        in_specs=(
            P("dp", None, "mp"),
            P(None, "dp", None, "mp"),
            P("dp", None, "mp"),
            P("dp"),
            P(),
            P(),
            P(("dp", "mp"), None, None, None),
            P(("dp", "mp"), None, None),
        ),
        out_specs=(
            P("dp", None, "mp"),
            P(None, "dp", None, "mp"),
            P(("dp", "mp"), None, None, None),
        ),
        check_vma=False,
    )
```

```python
import functools
import math

import jax
import jax.numpy as jnp
from jax import lax
from jax.experimental import pallas as pl
from jax.experimental.pallas import tpu as pltpu
from jax.sharding import PartitionSpec as P

DH = 128
LEAD_DP = 42
SMEM = pl.BlockSpec(memory_space=pltpu.SMEM)
VMEM = pl.BlockSpec(memory_space=pltpu.VMEM)
HBM = pl.BlockSpec(memory_space=pltpu.MemorySpace.HBM)
PARAMS = pltpu.CompilerParams(vmem_limit_bytes=48 * 1024 * 1024)
INV_ROOT = 1.0 / DH**0.5
TO_EXP2 = math.log2(math.e) / DH**0.5
ACROSS = (((1,), (1,)), ((), ()))


def scale_kernel(chunks, pages_ref, scales_ref, out_ref, pages, scales, scaled, in_sems, out_sems, scales_sem):
    rows = pages_ref.shape[0]
    groups, heads = scales_ref.shape
    step = rows // chunks
    parts = [pl.ds(c * step, step) for c in range(chunks)]
    arriving = [
        pltpu.make_async_copy(pages_ref.at[part], pages.at[part], in_sems.at[c])
        for c, part in enumerate(parts)
    ]
    leaving = [
        pltpu.make_async_copy(scaled.at[:, part], out_ref.at[:, part], out_sems.at[c])
        for c, part in enumerate(parts)
    ]
    scales_copy = pltpu.make_async_copy(scales_ref, scales, scales_sem)
    scales_copy.start()
    for copy in arriving:
        copy.start()
    scales_copy.wait()
    factors = scales[...].astype(jnp.float32)
    factors = jnp.broadcast_to(factors[:, None, :], (groups, rows // groups, heads)).reshape(rows, heads)
    for c in range(chunks):
        arriving[c].wait()
        for j in range(heads):
            stored = pages[c * step : (c + 1) * step, j * DH : (j + 1) * DH].astype(jnp.float32)
            factor = factors[c * step : (c + 1) * step, j : j + 1]
            scaled[j, c * step : (c + 1) * step] = (stored * factor).astype(jnp.bfloat16)
        leaving[c].start()
    for copy in leaving:
        copy.wait()


def index_kernel(send_ref, sum_ref, source_ref, send_out, sum_out, source_out):
    for i in range(send_ref.shape[0]):
        send_out[i] = send_ref[i]
        sum_out[i] = sum_ref[i]
    for i in range(source_ref.shape[0]):
        source_out[i] = source_ref[i]


def select_kernel(rows_ref, pages_ref, out_ref):
    for r in range(out_ref.shape[0]):
        out_ref[r] = pages_ref[rows_ref[r]]


def own_kernel(length_ref, own_ref, q_ref, g_ref, q_rows_ref, g_rows_ref, top_ref, sum_ref, dot_ref):
    resp_len = q_ref.shape[0]
    live = lax.broadcasted_iota(jnp.int32, (resp_len, DH), 0) < length_ref[0]
    key_pos = lax.broadcasted_iota(jnp.int32, (resp_len, resp_len), 0)
    row_pos = lax.broadcasted_iota(jnp.int32, (resp_len, resp_len), 1)
    for h in range(q_ref.shape[1] // DH):
        rows = slice(h * resp_len, (h + 1) * resp_len)
        q = q_ref[:, h * DH : (h + 1) * DH]
        g = g_ref[:, h * DH : (h + 1) * DH]
        g = jnp.where(live, g, jnp.zeros_like(g))
        q_rows_ref[rows] = q
        g_rows_ref[rows] = g
        scores = lax.dot_general(own_ref[0], q, ACROSS, preferred_element_type=jnp.float32)
        grad_weights = lax.dot_general(own_ref[1], g, ACROSS, preferred_element_type=jnp.float32)
        scores = jnp.where(key_pos <= row_pos, scores, -1e30)
        top = jnp.max(scores, axis=0, keepdims=True)
        exps = jnp.exp2((scores - top) * TO_EXP2)
        top_ref[:, rows] = top
        sum_ref[:, rows] = jnp.sum(exps, axis=0, keepdims=True)
        dot_ref[:, rows] = jnp.sum(exps * grad_weights, axis=0, keepdims=True)


def gather_pages(sources_ref, arrived_ref, key_ref, value_ref):
    page_rows = arrived_ref.shape[1] // 2
    for i in range(sources_ref.shape[0]):
        slot = sources_ref[i]
        rows = slice(i * page_rows, (i + 1) * page_rows)
        key_ref[rows] = arrived_ref[slot, :page_rows]
        value_ref[rows] = arrived_ref[slot, page_rows:]


def page_grad_kernel(
    sources_ref, arrived_ref, q_ref, g_ref, top_ref, sum_ref, dot_ref, sent_ref, key_ref, value_ref
):
    gather_pages(sources_ref, arrived_ref, key_ref, value_ref)
    q = q_ref[...]
    g = g_ref[...]
    scores = lax.dot_general(key_ref[...], q, ACROSS, preferred_element_type=jnp.float32)
    grad_weights = lax.dot_general(value_ref[...], g, ACROSS, preferred_element_type=jnp.float32)
    own_top = top_ref[...]
    top = jnp.maximum(jnp.max(scores, axis=0, keepdims=True), own_top)
    exps = jnp.exp2((scores - top) * TO_EXP2)
    back = jnp.exp2((own_top - top) * TO_EXP2)
    scale = 1.0 / (jnp.sum(exps, axis=0, keepdims=True) + back * sum_ref[...])
    delta = (jnp.sum(exps * grad_weights, axis=0, keepdims=True) + back * dot_ref[...]) * scale
    weights = exps * scale
    grad_scores = (weights * (grad_weights - delta)).astype(jnp.bfloat16)
    value_grad = jnp.dot(weights.astype(jnp.bfloat16), g, preferred_element_type=jnp.float32)
    key_grad = jnp.dot(grad_scores, q, preferred_element_type=jnp.float32) * INV_ROOT
    value_grad = value_grad.astype(jnp.bfloat16)
    key_grad = key_grad.astype(jnp.bfloat16)
    page_rows = arrived_ref.shape[1] // 2
    for i in range(sources_ref.shape[0]):
        slot = sources_ref[i]
        rows = slice(i * page_rows, (i + 1) * page_rows)
        sent_ref[slot, :page_rows] = key_grad[rows]
        sent_ref[slot, page_rows:] = value_grad[rows]


def own_grad_kernel(
    sources_ref, arrived_ref, own_ref, q_ref, g_ref, d_query_ref, d_own_ref, key_ref, value_ref
):
    resp_len = d_query_ref.shape[0]
    prompt_len = key_ref.shape[0] - resp_len
    gather_pages(sources_ref, arrived_ref, key_ref, value_ref)
    key_ref[prompt_len:] = own_ref[0]
    value_ref[prompt_len:] = own_ref[1]
    keys = key_ref[...]
    values = value_ref[...]
    keys_t = keys.astype(jnp.float32).T.astype(jnp.bfloat16)
    width = 2 * resp_len
    own_pos = lax.broadcasted_iota(jnp.int32, (resp_len, width), 0)
    row_pos = lax.broadcasted_iota(jnp.int32, (resp_len, width), 1) % resp_len
    allowed = own_pos <= row_pos
    key_grad = None
    value_grad = None
    for b in range(q_ref.shape[0] // width):
        q = q_ref[b * width : (b + 1) * width]
        g = g_ref[b * width : (b + 1) * width]
        scores = lax.dot_general(keys, q, ACROSS, preferred_element_type=jnp.float32)
        grad_weights = lax.dot_general(values, g, ACROSS, preferred_element_type=jnp.float32)
        own_scores = jnp.where(allowed, scores[prompt_len:], -1e30)
        scores = jnp.concatenate([scores[:prompt_len], own_scores], axis=0)
        exps = jnp.exp2((scores - jnp.max(scores, axis=0, keepdims=True)) * TO_EXP2)
        scale = 1.0 / jnp.sum(exps, axis=0, keepdims=True)
        delta = jnp.sum(exps * grad_weights, axis=0, keepdims=True) * scale
        weights = exps * scale
        grad_scores = (weights * (grad_weights - delta)).astype(jnp.bfloat16)
        own_weights = weights[prompt_len:].astype(jnp.bfloat16)
        part = jnp.dot(own_weights, g, preferred_element_type=jnp.float32)
        value_grad = part if value_grad is None else value_grad + part
        part = jnp.dot(grad_scores[prompt_len:], q, preferred_element_type=jnp.float32)
        key_grad = part if key_grad is None else key_grad + part
        d_q = jnp.dot(keys_t, grad_scores, preferred_element_type=jnp.float32) * INV_ROOT
        for k in range(2):
            head = 2 * b + k
            block = d_q[:, k * resp_len : (k + 1) * resp_len].T
            d_query_ref[:, head * DH : (head + 1) * DH] = block.astype(jnp.bfloat16)
    d_own_ref[0] = (key_grad * INV_ROOT).astype(jnp.bfloat16)
    d_own_ref[1] = value_grad.astype(jnp.bfloat16)


def sum_kernel(rows_ref, arrived_ref, out_ref, total_ref):
    pages = out_ref.shape[0]
    total_ref[...] = jnp.zeros_like(total_ref)
    for r in range(arrived_ref.shape[0]):
        row = rows_ref[r]
        total_ref[row] = total_ref[row] + arrived_ref[r].astype(jnp.float32)
    out_ref[...] = total_ref[:pages].astype(jnp.bfloat16)


def layout_kernel(parts_ref, out_ref):
    for j in range(parts_ref.shape[0]):
        out_ref[:, j * DH : (j + 1) * DH] = parts_ref[j].astype(jnp.float32)


def per_device(resp_q, resp_kv, d_out, lengths, fork, page_table, pool_pages, pool_scales):
    dp_size = lax.axis_size("dp")
    mp_size = lax.axis_size("mp")
    my_dp = lax.axis_index("dp")
    pool_dev, _, page_rows, _ = pool_pages.shape
    heads_kv = pool_scales.shape[-1]
    pages_prompt = page_table.shape[1]
    resp_len = resp_q.shape[1]
    q_rows_all = resp_len * (resp_q.shape[2] // DH)
    prompt_len = pages_prompt * page_rows
    total = prompt_len + resp_len
    group_rows = mp_size * pool_dev
    slot_rows = 2 * page_rows
    stored_rows = pool_dev * slot_rows
    bf16 = jnp.bfloat16

    chunks = 4
    by_head = pl.pallas_call(
        functools.partial(scale_kernel, chunks),
        out_shape=jax.ShapeDtypeStruct((heads_kv, stored_rows, DH), bf16),
        in_specs=[HBM, HBM],
        out_specs=HBM,
        scratch_shapes=[
            pltpu.VMEM((stored_rows, heads_kv * DH), bf16),
            pltpu.VMEM((pool_dev * 2, heads_kv), bf16),
            pltpu.VMEM((heads_kv, stored_rows, DH), bf16),
            pltpu.SemaphoreType.DMA((chunks,)),
            pltpu.SemaphoreType.DMA((chunks,)),
            pltpu.SemaphoreType.DMA,
        ],
    )(pool_pages.reshape(stored_rows, -1), pool_scales.reshape(pool_dev * 2, heads_kv))
    regrouped = lax.all_to_all(by_head, "mp", split_axis=0, concat_axis=0, tiled=True)
    regrouped = regrouped.reshape(group_rows, slot_rows, DH)

    wanted = jnp.take(page_table, fork, axis=0)
    on_device = wanted // group_rows == my_dp
    send_rows = jnp.sum(jnp.where(on_device, wanted % group_rows, 0), axis=1)
    sum_rows = jnp.where(jnp.any(on_device, axis=1), send_rows, group_rows)
    sources = jnp.take(wanted, my_dp, axis=0) // group_rows
    lead = LEAD_DP % dp_size
    order = [[(lead + k) % dp_size for k in range(dp_size)]]
    send_rows = jnp.roll(send_rows, -lead)
    sum_rows = jnp.roll(sum_rows, -lead)
    sources = (sources - lead) % dp_size
    send_rows, sum_rows, sources = pl.pallas_call(
        index_kernel,
        out_shape=tuple(pltpu.MemorySpace.SMEM(v.shape, v.dtype) for v in (send_rows, sum_rows, sources)),
        in_specs=[SMEM, SMEM, SMEM],
        out_specs=(SMEM, SMEM, SMEM),
        compiler_params=PARAMS,
    )(send_rows, sum_rows, sources)

    own = resp_kv[:, 0]
    rows = jax.ShapeDtypeStruct((q_rows_all, DH), bf16)
    stat = jax.ShapeDtypeStruct((1, q_rows_all), jnp.float32)
    q_rows, g_rows, *stats = pl.pallas_call(
        own_kernel,
        out_shape=(rows, rows, stat, stat, stat),
        in_specs=[SMEM, VMEM, VMEM, VMEM],
        out_specs=(VMEM,) * 5,
        compiler_params=PARAMS,
        cost_estimate=pl.CostEstimate(flops=10**8, bytes_accessed=2**21, transcendentals=2**17),
    )(lengths, own, resp_q[0], d_out[0])
    send_rows, q_rows, g_rows = lax.optimization_barrier((send_rows, q_rows, g_rows))

    slots = jax.ShapeDtypeStruct((dp_size, slot_rows, DH), bf16)
    selected = pl.pallas_call(
        select_kernel,
        out_shape=slots,
        in_specs=[SMEM, VMEM],
        out_specs=VMEM,
        compiler_params=PARAMS,
    )(send_rows, regrouped)
    arrived = lax.all_to_all(selected, "dp", split_axis=0, concat_axis=0, axis_index_groups=order, tiled=True)

    sent = pl.pallas_call(
        page_grad_kernel,
        out_shape=slots,
        in_specs=[SMEM] + [VMEM] * 6,
        out_specs=VMEM,
        scratch_shapes=[pltpu.VMEM((prompt_len, DH), bf16), pltpu.VMEM((prompt_len, DH), bf16)],
        compiler_params=PARAMS,
    )(sources, arrived, q_rows, g_rows, *stats)
    returned = lax.all_to_all(sent, "dp", split_axis=0, concat_axis=0, axis_index_groups=order, tiled=True)

    d_query, d_own = pl.pallas_call(
        own_grad_kernel,
        out_shape=(
            jax.ShapeDtypeStruct(resp_q.shape[1:], bf16),
            jax.ShapeDtypeStruct((2, resp_len, DH), bf16),
        ),
        in_specs=[SMEM] + [VMEM] * 4,
        out_specs=(VMEM, VMEM),
        scratch_shapes=[pltpu.VMEM((total, DH), bf16), pltpu.VMEM((total, DH), bf16)],
        compiler_params=PARAMS,
        cost_estimate=pl.CostEstimate(flops=2 * 10**9, bytes_accessed=2**22, transcendentals=2**20),
    )(sources, arrived, own, q_rows, g_rows)

    summed = pl.pallas_call(
        sum_kernel,
        out_shape=jax.ShapeDtypeStruct((group_rows, slot_rows, DH), bf16),
        in_specs=[SMEM, VMEM],
        out_specs=VMEM,
        scratch_shapes=[pltpu.VMEM((group_rows + 1, slot_rows, DH), jnp.float32)],
        compiler_params=PARAMS,
    )(sum_rows, returned)
    restored = lax.all_to_all(
        summed.reshape(mp_size, stored_rows, DH), "mp", split_axis=0, concat_axis=0, tiled=True
    )
    d_pool = pl.pallas_call(
        layout_kernel,
        out_shape=jax.ShapeDtypeStruct((stored_rows, heads_kv * DH), jnp.float32),
        in_specs=[VMEM],
        out_specs=VMEM,
        compiler_params=PARAMS,
    )(restored)
    return d_query[None], d_own[:, None], d_pool.reshape(pool_pages.shape)


def solution(mesh):
    return jax.shard_map(
        per_device,
        mesh=mesh,
        in_specs=(
            P("dp", None, "mp"),
            P(None, "dp", None, "mp"),
            P("dp", None, "mp"),
            P("dp"),
            P(),
            P(),
            P(("dp", "mp"), None, None, None),
            P(("dp", "mp"), None, None),
        ),
        out_specs=(
            P("dp", None, "mp"),
            P(None, "dp", None, "mp"),
            P(("dp", "mp"), None, None, None),
        ),
        check_vma=False,
    )
```

```python
import functools
import math

import jax
import jax.numpy as jnp
from jax import lax
from jax.experimental import pallas as pl
from jax.experimental.pallas import tpu as pltpu
from jax.sharding import PartitionSpec as P

DH = 128
LEAD_DP = 26
LEAD_MP = 4
SMEM = pl.BlockSpec(memory_space=pltpu.SMEM)
VMEM = pl.BlockSpec(memory_space=pltpu.VMEM)
HBM = pl.BlockSpec(memory_space=pltpu.MemorySpace.HBM)
PARAMS = pltpu.CompilerParams(vmem_limit_bytes=48 * 1024 * 1024)
INV_ROOT = 1.0 / DH**0.5
TO_EXP2 = math.log2(math.e) / DH**0.5
ACROSS = (((1,), (1,)), ((), ()))


def scale_kernel(
    chunks, order, pages_ref, scales_ref, out_ref, pages, scales, scaled, in_sems, out_sems, scales_sem
):
    rows = pages_ref.shape[0]
    groups, heads = scales_ref.shape
    step = rows // chunks
    parts = [pl.ds(c * step, step) for c in range(chunks)]
    arriving = [
        pltpu.make_async_copy(pages_ref.at[part], pages.at[part], in_sems.at[c])
        for c, part in enumerate(parts)
    ]
    leaving = [
        pltpu.make_async_copy(scaled.at[:, part], out_ref.at[:, part], out_sems.at[c])
        for c, part in enumerate(parts)
    ]
    scales_copy = pltpu.make_async_copy(scales_ref, scales, scales_sem)
    scales_copy.start()
    for copy in arriving:
        copy.start()
    scales_copy.wait()
    factors = scales[...].astype(jnp.float32)
    factors = jnp.broadcast_to(factors[:, None, :], (groups, rows // groups, heads)).reshape(rows, heads)
    for c in range(chunks):
        arriving[c].wait()
        for k, j in enumerate(order):
            stored = pages[c * step : (c + 1) * step, j * DH : (j + 1) * DH].astype(jnp.float32)
            factor = factors[c * step : (c + 1) * step, j : j + 1]
            scaled[k, c * step : (c + 1) * step] = (stored * factor).astype(jnp.bfloat16)
        leaving[c].start()
    for copy in leaving:
        copy.wait()


def dp_order(size):
    return [(LEAD_DP + k) % size for k in range(size)]


def mp_order(size):
    return [(LEAD_MP + k) % size for k in range(size)]


def index_kernel(order, shift, send_ref, found_ref, source_ref, place_ref, send_out, sum_out, source_out):
    pages = len(order)
    for k, r in enumerate(order):
        row = lax.rem(send_ref[r] + shift, pages)
        send_out[k] = row
        sum_out[k] = jnp.where(found_ref[r] > 0, row, pages)
    for i in range(source_ref.shape[0]):
        source_out[i] = place_ref[source_ref[i]]


def select_kernel(rows_ref, pages_ref, out_ref):
    for r in range(out_ref.shape[0]):
        out_ref[r] = pages_ref[rows_ref[r]]


def own_kernel(length_ref, own_ref, q_ref, g_ref, q_rows_ref, g_rows_ref, top_ref, sum_ref, dot_ref):
    resp_len = q_ref.shape[0]
    live = lax.broadcasted_iota(jnp.int32, (resp_len, DH), 0) < length_ref[0]
    key_pos = lax.broadcasted_iota(jnp.int32, (resp_len, resp_len), 0)
    row_pos = lax.broadcasted_iota(jnp.int32, (resp_len, resp_len), 1)
    for h in range(q_ref.shape[1] // DH):
        rows = slice(h * resp_len, (h + 1) * resp_len)
        q = q_ref[:, h * DH : (h + 1) * DH]
        g = g_ref[:, h * DH : (h + 1) * DH]
        g = jnp.where(live, g, jnp.zeros_like(g))
        q_rows_ref[rows] = q
        g_rows_ref[rows] = g
        scores = lax.dot_general(own_ref[0], q, ACROSS, preferred_element_type=jnp.float32)
        grad_weights = lax.dot_general(own_ref[1], g, ACROSS, preferred_element_type=jnp.float32)
        scores = jnp.where(key_pos <= row_pos, scores, -1e30)
        top = jnp.max(scores, axis=0, keepdims=True)
        exps = jnp.exp2((scores - top) * TO_EXP2)
        top_ref[:, rows] = top
        sum_ref[:, rows] = jnp.sum(exps, axis=0, keepdims=True)
        dot_ref[:, rows] = jnp.sum(exps * grad_weights, axis=0, keepdims=True)


def gather_pages(sources_ref, arrived_ref, key_ref, value_ref):
    page_rows = arrived_ref.shape[1] // 2
    for i in range(sources_ref.shape[0]):
        slot = sources_ref[i]
        rows = slice(i * page_rows, (i + 1) * page_rows)
        key_ref[rows] = arrived_ref[slot, :page_rows]
        value_ref[rows] = arrived_ref[slot, page_rows:]


def page_grad_kernel(
    sources_ref, arrived_ref, q_ref, g_ref, top_ref, sum_ref, dot_ref, sent_ref, key_ref, value_ref
):
    gather_pages(sources_ref, arrived_ref, key_ref, value_ref)
    q = q_ref[...]
    g = g_ref[...]
    scores = lax.dot_general(key_ref[...], q, ACROSS, preferred_element_type=jnp.float32)
    grad_weights = lax.dot_general(value_ref[...], g, ACROSS, preferred_element_type=jnp.float32)
    own_top = top_ref[...]
    top = jnp.maximum(jnp.max(scores, axis=0, keepdims=True), own_top)
    exps = jnp.exp2((scores - top) * TO_EXP2)
    back = jnp.exp2((own_top - top) * TO_EXP2)
    scale = 1.0 / (jnp.sum(exps, axis=0, keepdims=True) + back * sum_ref[...])
    delta = (jnp.sum(exps * grad_weights, axis=0, keepdims=True) + back * dot_ref[...]) * scale
    weights = exps * scale
    grad_scores = (weights * (grad_weights - delta)).astype(jnp.bfloat16)
    value_grad = jnp.dot(weights.astype(jnp.bfloat16), g, preferred_element_type=jnp.float32)
    key_grad = jnp.dot(grad_scores, q, preferred_element_type=jnp.float32) * INV_ROOT
    value_grad = value_grad.astype(jnp.bfloat16)
    key_grad = key_grad.astype(jnp.bfloat16)
    page_rows = arrived_ref.shape[1] // 2
    for i in range(sources_ref.shape[0]):
        slot = sources_ref[i]
        rows = slice(i * page_rows, (i + 1) * page_rows)
        sent_ref[slot, :page_rows] = key_grad[rows]
        sent_ref[slot, page_rows:] = value_grad[rows]


def own_grad_kernel(
    sources_ref, arrived_ref, own_ref, q_ref, g_ref, d_query_ref, d_own_ref, key_ref, value_ref
):
    resp_len = d_query_ref.shape[0]
    prompt_len = key_ref.shape[0] - resp_len
    gather_pages(sources_ref, arrived_ref, key_ref, value_ref)
    key_ref[prompt_len:] = own_ref[0]
    value_ref[prompt_len:] = own_ref[1]
    keys = key_ref[...]
    values = value_ref[...]
    keys_t = keys.astype(jnp.float32).T.astype(jnp.bfloat16)
    width = 2 * resp_len
    own_pos = lax.broadcasted_iota(jnp.int32, (resp_len, width), 0)
    row_pos = lax.broadcasted_iota(jnp.int32, (resp_len, width), 1) % resp_len
    allowed = own_pos <= row_pos
    key_grad = None
    value_grad = None
    for b in range(q_ref.shape[0] // width):
        q = q_ref[b * width : (b + 1) * width]
        g = g_ref[b * width : (b + 1) * width]
        scores = lax.dot_general(keys, q, ACROSS, preferred_element_type=jnp.float32)
        grad_weights = lax.dot_general(values, g, ACROSS, preferred_element_type=jnp.float32)
        own_scores = jnp.where(allowed, scores[prompt_len:], -1e30)
        scores = jnp.concatenate([scores[:prompt_len], own_scores], axis=0)
        exps = jnp.exp2((scores - jnp.max(scores, axis=0, keepdims=True)) * TO_EXP2)
        scale = 1.0 / jnp.sum(exps, axis=0, keepdims=True)
        delta = jnp.sum(exps * grad_weights, axis=0, keepdims=True) * scale
        weights = exps * scale
        grad_scores = (weights * (grad_weights - delta)).astype(jnp.bfloat16)
        own_weights = weights[prompt_len:].astype(jnp.bfloat16)
        part = jnp.dot(own_weights, g, preferred_element_type=jnp.float32)
        value_grad = part if value_grad is None else value_grad + part
        part = jnp.dot(grad_scores[prompt_len:], q, preferred_element_type=jnp.float32)
        key_grad = part if key_grad is None else key_grad + part
        d_q = jnp.dot(keys_t, grad_scores, preferred_element_type=jnp.float32) * INV_ROOT
        for k in range(2):
            head = 2 * b + k
            block = d_q[:, k * resp_len : (k + 1) * resp_len].T
            d_query_ref[:, head * DH : (head + 1) * DH] = block.astype(jnp.bfloat16)
    d_own_ref[0] = (key_grad * INV_ROOT).astype(jnp.bfloat16)
    d_own_ref[1] = value_grad.astype(jnp.bfloat16)


def sum_kernel(rows_ref, arrived_ref, out_ref, total_ref):
    pages = out_ref.shape[0]
    total_ref[...] = jnp.zeros_like(total_ref)
    for r in range(arrived_ref.shape[0]):
        row = rows_ref[r]
        total_ref[row] = total_ref[row] + arrived_ref[r].astype(jnp.float32)
    out_ref[...] = total_ref[:pages].astype(jnp.bfloat16)


def layout_kernel(order, parts_ref, out_ref):
    for k, j in enumerate(order):
        out_ref[:, j * DH : (j + 1) * DH] = parts_ref[k].astype(jnp.float32)


def exchange(parts, axis, order):
    return lax.all_to_all(
        parts, axis, split_axis=0, concat_axis=0, axis_index_groups=[order], tiled=True
    )


def per_device(resp_q, resp_kv, d_out, lengths, fork, page_table, pool_pages, pool_scales):
    dp_size = lax.axis_size("dp")
    mp_size = lax.axis_size("mp")
    my_dp = lax.axis_index("dp")
    pool_dev, _, page_rows, _ = pool_pages.shape
    heads_kv = pool_scales.shape[-1]
    pages_prompt = page_table.shape[1]
    resp_len = resp_q.shape[1]
    q_rows_all = resp_len * (resp_q.shape[2] // DH)
    prompt_len = pages_prompt * page_rows
    total = prompt_len + resp_len
    group_rows = mp_size * pool_dev
    slot_rows = 2 * page_rows
    stored_rows = pool_dev * slot_rows
    bf16 = jnp.bfloat16

    order = dp_order(dp_size)
    heads = mp_order(mp_size)

    chunks = 4
    by_head = pl.pallas_call(
        functools.partial(scale_kernel, chunks, heads),
        out_shape=jax.ShapeDtypeStruct((heads_kv, stored_rows, DH), bf16),
        in_specs=[HBM, HBM],
        out_specs=HBM,
        scratch_shapes=[
            pltpu.VMEM((stored_rows, heads_kv * DH), bf16),
            pltpu.VMEM((pool_dev * 2, heads_kv), bf16),
            pltpu.VMEM((heads_kv, stored_rows, DH), bf16),
            pltpu.SemaphoreType.DMA((chunks,)),
            pltpu.SemaphoreType.DMA((chunks,)),
            pltpu.SemaphoreType.DMA,
        ],
    )(pool_pages.reshape(stored_rows, -1), pool_scales.reshape(pool_dev * 2, heads_kv))
    regrouped = exchange(by_head, "mp", heads)
    regrouped = regrouped.reshape(group_rows, slot_rows, DH)

    wanted = jnp.take(page_table, fork, axis=0)
    on_device = wanted // group_rows == my_dp
    send_rows = jnp.sum(jnp.where(on_device, wanted % group_rows, 0), axis=1)
    found = jnp.sum(on_device.astype(jnp.int32), axis=1)
    sources = jnp.take(wanted, my_dp, axis=0) // group_rows
    place = jnp.asarray([order.index(d) for d in range(dp_size)], jnp.int32)
    send_rows, sum_rows, sources = pl.pallas_call(
        functools.partial(index_kernel, order, group_rows - heads[0] * pool_dev),
        out_shape=tuple(pltpu.MemorySpace.SMEM(v.shape, v.dtype) for v in (send_rows, found, sources)),
        in_specs=[SMEM, SMEM, SMEM, SMEM],
        out_specs=(SMEM, SMEM, SMEM),
        compiler_params=PARAMS,
    )(send_rows, found, sources, place)

    own = resp_kv[:, 0]
    rows = jax.ShapeDtypeStruct((q_rows_all, DH), bf16)
    stat = jax.ShapeDtypeStruct((1, q_rows_all), jnp.float32)
    q_rows, g_rows, *stats = pl.pallas_call(
        own_kernel,
        out_shape=(rows, rows, stat, stat, stat),
        in_specs=[SMEM, VMEM, VMEM, VMEM],
        out_specs=(VMEM,) * 5,
        compiler_params=PARAMS,
        cost_estimate=pl.CostEstimate(flops=10**8, bytes_accessed=2**21, transcendentals=2**17),
    )(lengths, own, resp_q[0], d_out[0])
    send_rows, q_rows, g_rows = lax.optimization_barrier((send_rows, q_rows, g_rows))

    slots = jax.ShapeDtypeStruct((dp_size, slot_rows, DH), bf16)
    selected = pl.pallas_call(
        select_kernel,
        out_shape=slots,
        in_specs=[SMEM, VMEM],
        out_specs=VMEM,
        compiler_params=PARAMS,
    )(send_rows, regrouped)
    arrived = exchange(selected, "dp", order)

    sent = pl.pallas_call(
        page_grad_kernel,
        out_shape=slots,
        in_specs=[SMEM] + [VMEM] * 6,
        out_specs=VMEM,
        scratch_shapes=[pltpu.VMEM((prompt_len, DH), bf16), pltpu.VMEM((prompt_len, DH), bf16)],
        compiler_params=PARAMS,
    )(sources, arrived, q_rows, g_rows, *stats)
    returned = exchange(sent, "dp", order)

    d_query, d_own = pl.pallas_call(
        own_grad_kernel,
        out_shape=(
            jax.ShapeDtypeStruct(resp_q.shape[1:], bf16),
            jax.ShapeDtypeStruct((2, resp_len, DH), bf16),
        ),
        in_specs=[SMEM] + [VMEM] * 4,
        out_specs=(VMEM, VMEM),
        scratch_shapes=[pltpu.VMEM((total, DH), bf16), pltpu.VMEM((total, DH), bf16)],
        compiler_params=PARAMS,
        cost_estimate=pl.CostEstimate(flops=2 * 10**9, bytes_accessed=2**22, transcendentals=2**20),
    )(sources, arrived, own, q_rows, g_rows)

    summed = pl.pallas_call(
        sum_kernel,
        out_shape=jax.ShapeDtypeStruct((group_rows, slot_rows, DH), bf16),
        in_specs=[SMEM, VMEM],
        out_specs=VMEM,
        scratch_shapes=[pltpu.VMEM((group_rows + 1, slot_rows, DH), jnp.float32)],
        compiler_params=PARAMS,
    )(sum_rows, returned)
    restored = exchange(summed.reshape(mp_size, stored_rows, DH), "mp", heads)
    d_pool = pl.pallas_call(
        functools.partial(layout_kernel, heads),
        out_shape=jax.ShapeDtypeStruct((stored_rows, heads_kv * DH), jnp.float32),
        in_specs=[VMEM],
        out_specs=VMEM,
        compiler_params=PARAMS,
    )(restored)
    return d_query[None], d_own[:, None], d_pool.reshape(pool_pages.shape)


def solution(mesh):
    return jax.shard_map(
        per_device,
        mesh=mesh,
        in_specs=(
            P("dp", None, "mp"),
            P(None, "dp", None, "mp"),
            P("dp", None, "mp"),
            P("dp"),
            P(),
            P(),
            P(("dp", "mp"), None, None, None),
            P(("dp", "mp"), None, None),
        ),
        out_specs=(
            P("dp", None, "mp"),
            P(None, "dp", None, "mp"),
            P(("dp", "mp"), None, None, None),
        ),
        check_vma=False,
    )
```

```python
import functools
import math

import jax
import jax.numpy as jnp
from jax import lax
from jax.experimental import pallas as pl
from jax.experimental.pallas import tpu as pltpu
from jax.sharding import PartitionSpec as P

DH = 128
LEAD_DP = 27
LEAD_MP = 4
SMEM = pl.BlockSpec(memory_space=pltpu.SMEM)
VMEM = pl.BlockSpec(memory_space=pltpu.VMEM)
HBM = pl.BlockSpec(memory_space=pltpu.MemorySpace.HBM)
PARAMS = pltpu.CompilerParams(vmem_limit_bytes=48 * 1024 * 1024)
INV_ROOT = 1.0 / DH**0.5
TO_EXP2 = math.log2(math.e) / DH**0.5
ACROSS = (((1,), (1,)), ((), ()))


def scale_kernel(
    chunks, lists, pages_ref, scales_ref, *refs
):
    (out0_ref, out1_ref, pages, scales, scaled0, scaled1, in_sems, out_sems, scales_sem) = refs
    rows = pages_ref.shape[0]
    groups, heads = scales_ref.shape
    step = rows // chunks
    parts = [pl.ds(c * step, step) for c in range(chunks)]
    arriving = [
        pltpu.make_async_copy(pages_ref.at[part], pages.at[part], in_sems.at[c])
        for c, part in enumerate(parts)
    ]
    outs = [(scaled0, out0_ref), (scaled1, out1_ref)]
    leaving = [
        pltpu.make_async_copy(scaled.at[:, part], out_ref.at[:, part], out_sems.at[core, c])
        for core, (scaled, out_ref) in enumerate(outs)
        for c, part in enumerate(parts)
    ]
    scales_copy = pltpu.make_async_copy(scales_ref, scales, scales_sem)
    scales_copy.start()
    for copy in arriving:
        copy.start()
    scales_copy.wait()
    factors = scales[...].astype(jnp.float32)
    factors = jnp.broadcast_to(factors[:, None, :], (groups, rows // groups, heads)).reshape(rows, heads)
    for c in range(chunks):
        arriving[c].wait()
        for core, (scaled, _) in enumerate(outs):
            for k, j in enumerate(lists[core]):
                stored = pages[c * step : (c + 1) * step, j * DH : (j + 1) * DH].astype(jnp.float32)
                factor = factors[c * step : (c + 1) * step, j : j + 1]
                scaled[k, c * step : (c + 1) * step] = (stored * factor).astype(jnp.bfloat16)
            leaving[core * chunks + c].start()
    for copy in leaving:
        copy.wait()


def dp_order(size):
    return [(LEAD_DP + k) % size for k in range(size)]


def mp_order(size):
    return [(LEAD_MP + k) % size for k in range(size)]


def index_kernel(order, send_ref, sum_ref, source_ref, send_out, sum_out, source_out):
    for k, r in enumerate(order):
        send_out[k] = send_ref[r]
        sum_out[k] = sum_ref[r]
    for i in range(source_ref.shape[0]):
        source_out[i] = source_ref[i]


def select_kernel(rows_ref, first_ref, second_ref, out_ref):
    half = first_ref.shape[0]
    for r in range(out_ref.shape[0]):
        row = rows_ref[r]
        place = lax.rem(row, half)
        out_ref[r] = jnp.where(row < half, first_ref[place], second_ref[place])


def select_chips_kernel(pages_dev, chip_ref, rows_ref, *refs):
    *arrived_refs, out_ref, pages_ref = refs
    chips = len(arrived_refs)
    for d in range(chips):
        pages_ref[d] = arrived_refs[d][...]
    half = chips * pages_dev
    for r in range(out_ref.shape[0]):
        row = rows_ref[r]
        core = lax.div(row, half)
        place = lax.rem(row, half)
        back = lax.rem(chip_ref[0] + chips - lax.div(place, pages_dev), chips)
        out_ref[r] = pages_ref[back, core * pages_dev + lax.rem(place, pages_dev)]


def pair_kernel(chip_ref, first_ref, second_ref, *out_refs):
    chips = len(out_refs)
    for d in range(chips):
        chip = lax.rem(chip_ref[0] + d, chips)
        out_refs[d][0] = first_ref[chip]
        out_refs[d][1] = second_ref[chip]


def own_kernel(
    length_ref, own_ref, q_ref, g_ref, q_rows_ref, g_rows_ref, top_ref, sum_ref, exps_ref, grad_ref
):
    resp_len = q_ref.shape[0]
    live = lax.broadcasted_iota(jnp.int32, (resp_len, DH), 0) < length_ref[0]
    key_pos = lax.broadcasted_iota(jnp.int32, (resp_len, resp_len), 0)
    row_pos = lax.broadcasted_iota(jnp.int32, (resp_len, resp_len), 1)
    for h in range(q_ref.shape[1] // DH):
        rows = slice(h * resp_len, (h + 1) * resp_len)
        q = q_ref[:, h * DH : (h + 1) * DH]
        g = g_ref[:, h * DH : (h + 1) * DH]
        g = jnp.where(live, g, jnp.zeros_like(g))
        q_rows_ref[rows] = q
        g_rows_ref[rows] = g
        scores = lax.dot_general(own_ref[0], q, ACROSS, preferred_element_type=jnp.float32)
        grad_weights = lax.dot_general(own_ref[1], g, ACROSS, preferred_element_type=jnp.float32)
        scores = jnp.where(key_pos <= row_pos, scores, -1e30)
        top = jnp.max(scores, axis=0, keepdims=True)
        exps = jnp.exp2((scores - top) * TO_EXP2)
        top_ref[:, rows] = top
        sum_ref[:, rows] = jnp.sum(exps, axis=0, keepdims=True)
        exps_ref[:, rows] = exps
        grad_ref[:, rows] = grad_weights


def gather_pages(sources_ref, arrived_ref, key_ref, value_ref):
    page_rows = arrived_ref.shape[1] // 2
    for i in range(sources_ref.shape[0]):
        slot = sources_ref[i]
        rows = slice(i * page_rows, (i + 1) * page_rows)
        key_ref[rows] = arrived_ref[slot, :page_rows]
        value_ref[rows] = arrived_ref[slot, page_rows:]


def page_grad_kernel(
    sources_ref,
    arrived_ref,
    q_ref,
    g_ref,
    top_ref,
    sum_ref,
    own_exps_ref,
    own_grad_ref,
    sent_ref,
    key_ref,
    value_ref,
):
    gather_pages(sources_ref, arrived_ref, key_ref, value_ref)
    q = q_ref[...]
    g = g_ref[...]
    scores = lax.dot_general(key_ref[...], q, ACROSS, preferred_element_type=jnp.float32)
    grad_weights = lax.dot_general(value_ref[...], g, ACROSS, preferred_element_type=jnp.float32)
    own_top = top_ref[...]
    top = jnp.maximum(jnp.max(scores, axis=0, keepdims=True), own_top)
    exps = jnp.exp2((scores - top) * TO_EXP2)
    back = jnp.exp2((own_top - top) * TO_EXP2)
    scale = 1.0 / (jnp.sum(exps, axis=0, keepdims=True) + back * sum_ref[...])
    weights = exps * scale
    weights_b = weights.astype(jnp.bfloat16)
    own_weights = (own_exps_ref[...] * (back * scale)).astype(jnp.bfloat16)
    delta = jnp.sum(weights_b.astype(jnp.float32) * grad_weights, axis=0, keepdims=True)
    delta += jnp.sum(own_weights.astype(jnp.float32) * own_grad_ref[...], axis=0, keepdims=True)
    grad_scores = (weights * (grad_weights - delta)).astype(jnp.bfloat16)
    value_grad = jnp.dot(weights_b, g, preferred_element_type=jnp.float32)
    key_grad = jnp.dot(grad_scores, q, preferred_element_type=jnp.float32) * INV_ROOT
    value_grad = value_grad.astype(jnp.bfloat16)
    key_grad = key_grad.astype(jnp.bfloat16)
    page_rows = arrived_ref.shape[1] // 2
    for i in range(sources_ref.shape[0]):
        slot = sources_ref[i]
        rows = slice(i * page_rows, (i + 1) * page_rows)
        sent_ref[slot, :page_rows] = key_grad[rows]
        sent_ref[slot, page_rows:] = value_grad[rows]


def own_grad_kernel(
    sources_ref, arrived_ref, own_ref, q_ref, g_ref, d_query_ref, d_own_ref, key_ref, value_ref
):
    resp_len = d_query_ref.shape[0]
    prompt_len = key_ref.shape[0] - resp_len
    gather_pages(sources_ref, arrived_ref, key_ref, value_ref)
    key_ref[prompt_len:] = own_ref[0]
    value_ref[prompt_len:] = own_ref[1]
    keys = key_ref[...]
    values = value_ref[...]
    keys_t = keys.astype(jnp.float32).T.astype(jnp.bfloat16)
    width = 2 * resp_len
    own_pos = lax.broadcasted_iota(jnp.int32, (resp_len, width), 0)
    row_pos = lax.broadcasted_iota(jnp.int32, (resp_len, width), 1) % resp_len
    allowed = own_pos <= row_pos
    key_grad = None
    value_grad = None
    for b in range(q_ref.shape[0] // width):
        q = q_ref[b * width : (b + 1) * width]
        g = g_ref[b * width : (b + 1) * width]
        scores = lax.dot_general(keys, q, ACROSS, preferred_element_type=jnp.float32)
        grad_weights = lax.dot_general(values, g, ACROSS, preferred_element_type=jnp.float32)
        own_scores = jnp.where(allowed, scores[prompt_len:], -1e30)
        scores = jnp.concatenate([scores[:prompt_len], own_scores], axis=0)
        exps = jnp.exp2((scores - jnp.max(scores, axis=0, keepdims=True)) * TO_EXP2)
        scale = 1.0 / jnp.sum(exps, axis=0, keepdims=True)
        weights = exps * scale
        weights_b = weights.astype(jnp.bfloat16)
        delta = jnp.sum(weights_b.astype(jnp.float32) * grad_weights, axis=0, keepdims=True)
        grad_scores = (weights * (grad_weights - delta)).astype(jnp.bfloat16)
        part = jnp.dot(weights_b[prompt_len:], g, preferred_element_type=jnp.float32)
        value_grad = part if value_grad is None else value_grad + part
        part = jnp.dot(grad_scores[prompt_len:], q, preferred_element_type=jnp.float32)
        key_grad = part if key_grad is None else key_grad + part
        d_q = jnp.dot(keys_t, grad_scores, preferred_element_type=jnp.float32) * INV_ROOT
        for k in range(2):
            head = 2 * b + k
            block = d_q[:, k * resp_len : (k + 1) * resp_len].T
            d_query_ref[:, head * DH : (head + 1) * DH] = block.astype(jnp.bfloat16)
    d_own_ref[0] = (key_grad * INV_ROOT).astype(jnp.bfloat16)
    d_own_ref[1] = value_grad.astype(jnp.bfloat16)


def sum_kernel(rows_ref, arrived_ref, out_ref, total_ref):
    pages = out_ref.shape[0]
    total_ref[...] = jnp.zeros_like(total_ref)
    for r in range(arrived_ref.shape[0]):
        row = rows_ref[r]
        total_ref[row] = total_ref[row] + arrived_ref[r].astype(jnp.float32)
    out_ref[...] = total_ref[:pages].astype(jnp.bfloat16)


def layout_kernel(order, parts_ref, out_ref):
    for k, j in enumerate(order):
        out_ref[:, j * DH : (j + 1) * DH] = parts_ref[k].astype(jnp.float32)


def exchange(parts, axis, *groups):
    return lax.all_to_all(
        parts, axis, split_axis=0, concat_axis=0, axis_index_groups=list(groups), tiled=True
    )


def per_device(resp_q, resp_kv, d_out, lengths, fork, page_table, pool_pages, pool_scales):
    dp_size = lax.axis_size("dp")
    mp_size = lax.axis_size("mp")
    my_dp = lax.axis_index("dp")
    pool_dev, _, page_rows, _ = pool_pages.shape
    heads_kv = pool_scales.shape[-1]
    pages_prompt = page_table.shape[1]
    resp_len = resp_q.shape[1]
    q_rows_all = resp_len * (resp_q.shape[2] // DH)
    prompt_len = pages_prompt * page_rows
    total = prompt_len + resp_len
    group_rows = mp_size * pool_dev
    slot_rows = 2 * page_rows
    stored_rows = pool_dev * slot_rows
    bf16 = jnp.bfloat16

    order = dp_order(dp_size)
    heads = mp_order(mp_size)

    chunks = 4
    chips = mp_size // 2
    first_y = heads[0] // 2
    chip_order = [(first_y + k) % chips for k in range(chips)]
    lists = [[2 * y + core for y in chip_order] for core in range(2)]
    head_parts = jax.ShapeDtypeStruct((chips, stored_rows, DH), bf16)
    of_core0, of_core1 = pl.pallas_call(
        functools.partial(scale_kernel, chunks, lists),
        out_shape=(head_parts, head_parts),
        in_specs=[HBM, HBM],
        out_specs=(HBM, HBM),
        scratch_shapes=[
            pltpu.VMEM((stored_rows, heads_kv * DH), bf16),
            pltpu.VMEM((pool_dev * 2, heads_kv), bf16),
            pltpu.VMEM((chips, stored_rows, DH), bf16),
            pltpu.VMEM((chips, stored_rows, DH), bf16),
            pltpu.SemaphoreType.DMA((chunks,)),
            pltpu.SemaphoreType.DMA((2, chunks)),
            pltpu.SemaphoreType.DMA,
        ],
    )(pool_pages.reshape(stored_rows, -1), pool_scales.reshape(pool_dev * 2, heads_kv))
    from_core0 = lax.ppermute(of_core1, "mp", [(2 * y, 2 * y + 1) for y in range(chips)])
    along_y = exchange(of_core0, "mp", *lists)
    wanted = jnp.take(page_table, fork, axis=0)
    on_device = wanted // group_rows == my_dp
    send_rows = jnp.sum(jnp.where(on_device, wanted % group_rows, 0), axis=1)
    sum_rows = (send_rows + (group_rows - heads[0] * pool_dev)) % group_rows
    sum_rows = jnp.where(jnp.any(on_device, axis=1), sum_rows, group_rows)
    owner = send_rows // pool_dev
    chip = (owner // 2 + (chips - first_y)) % chips
    send_rows = owner % 2 * (group_rows // 2) + chip * pool_dev + send_rows % pool_dev
    sources = jnp.take(wanted, my_dp, axis=0) // group_rows
    sources = (sources + (dp_size - order[0])) % dp_size
    send_rows, sum_rows, sources = pl.pallas_call(
        functools.partial(index_kernel, order),
        out_shape=tuple(pltpu.MemorySpace.SMEM(v.shape, v.dtype) for v in (send_rows, sum_rows, sources)),
        in_specs=[SMEM, SMEM, SMEM],
        out_specs=(SMEM, SMEM, SMEM),
        compiler_params=PARAMS,
    )(send_rows, sum_rows, sources)

    own = resp_kv[:, 0]
    rows = jax.ShapeDtypeStruct((q_rows_all, DH), bf16)
    stat = jax.ShapeDtypeStruct((1, q_rows_all), jnp.float32)
    own_part = jax.ShapeDtypeStruct((resp_len, q_rows_all), jnp.float32)
    q_rows, g_rows, *stats = pl.pallas_call(
        own_kernel,
        out_shape=(rows, rows, stat, stat, own_part, own_part),
        in_specs=[SMEM, VMEM, VMEM, VMEM],
        out_specs=(VMEM,) * 6,
        compiler_params=PARAMS,
        cost_estimate=pl.CostEstimate(flops=10**8, bytes_accessed=2**21, transcendentals=2**17),
    )(lengths, own, resp_q[0], d_out[0])
    along_y, send_rows, q_rows, g_rows = lax.optimization_barrier((along_y, send_rows, q_rows, g_rows))
    from_core1 = lax.ppermute(along_y, "mp", [(2 * y + 1, 2 * y) for y in range(chips)])

    slots = jax.ShapeDtypeStruct((dp_size, slot_rows, DH), bf16)

    def core0(rows, own_pages, other_pages, own_heads, other_heads):
        selected = pl.pallas_call(
            select_kernel,
            out_shape=slots,
            in_specs=[SMEM, VMEM, VMEM],
            out_specs=VMEM,
            compiler_params=PARAMS,
        )(
            rows,
            own_pages.reshape(group_rows // 2, slot_rows, DH),
            other_pages.reshape(group_rows // 2, slot_rows, DH),
        )
        return exchange(selected, "dp", order)

    def core1(rows, own_pages, other_pages, own_heads, other_heads):
        chip = ((lax.axis_index("mp") // 2 + (chips - first_y)) % chips).reshape(1)
        parts = pl.pallas_call(
            pair_kernel,
            out_shape=(jax.ShapeDtypeStruct((2, stored_rows, DH), bf16),) * chips,
            in_specs=[SMEM, VMEM, VMEM],
            out_specs=(VMEM,) * chips,
            compiler_params=PARAMS,
        )(chip, other_heads, own_heads)
        moved = [parts[0]]
        for d in range(1, chips):
            pairs = [(2 * y + 1, 2 * ((y + d) % chips) + 1) for y in range(chips)]
            moved.append(lax.ppermute(parts[d], "mp", pairs))
        selected = pl.pallas_call(
            functools.partial(select_chips_kernel, pool_dev),
            out_shape=slots,
            in_specs=[SMEM, SMEM] + [VMEM] * chips,
            out_specs=VMEM,
            scratch_shapes=[pltpu.VMEM((chips, 2 * pool_dev, slot_rows, DH), bf16)],
            compiler_params=PARAMS,
        )(chip, rows, *[v.reshape(2 * pool_dev, slot_rows, DH) for v in moved])
        return exchange(selected, "dp", order)

    arrived = lax.cond(
        lax.axis_index("mp") % 2 == 0,
        core0,
        core1,
        send_rows,
        along_y,
        from_core1,
        of_core1,
        from_core0,
    )

    sent = pl.pallas_call(
        page_grad_kernel,
        out_shape=slots,
        in_specs=[SMEM] + [VMEM] * 7,
        out_specs=VMEM,
        scratch_shapes=[pltpu.VMEM((prompt_len, DH), bf16), pltpu.VMEM((prompt_len, DH), bf16)],
        compiler_params=PARAMS,
    )(sources, arrived, q_rows, g_rows, *stats)
    returned = exchange(sent, "dp", order)

    d_query, d_own = pl.pallas_call(
        own_grad_kernel,
        out_shape=(
            jax.ShapeDtypeStruct(resp_q.shape[1:], bf16),
            jax.ShapeDtypeStruct((2, resp_len, DH), bf16),
        ),
        in_specs=[SMEM] + [VMEM] * 4,
        out_specs=(VMEM, VMEM),
        scratch_shapes=[pltpu.VMEM((total, DH), bf16), pltpu.VMEM((total, DH), bf16)],
        compiler_params=PARAMS,
        cost_estimate=pl.CostEstimate(flops=2 * 10**9, bytes_accessed=2**22, transcendentals=2**20),
    )(sources, arrived, own, q_rows, g_rows)

    summed = pl.pallas_call(
        sum_kernel,
        out_shape=jax.ShapeDtypeStruct((group_rows, slot_rows, DH), bf16),
        in_specs=[SMEM, VMEM],
        out_specs=VMEM,
        scratch_shapes=[pltpu.VMEM((group_rows + 1, slot_rows, DH), jnp.float32)],
        compiler_params=PARAMS,
    )(sum_rows, returned)
    restored = exchange(summed.reshape(mp_size, stored_rows, DH), "mp", heads)
    d_pool = pl.pallas_call(
        functools.partial(layout_kernel, heads),
        out_shape=jax.ShapeDtypeStruct((stored_rows, heads_kv * DH), jnp.float32),
        in_specs=[VMEM],
        out_specs=VMEM,
        compiler_params=PARAMS,
    )(restored)
    return d_query[None], d_own[:, None], d_pool.reshape(pool_pages.shape)


def solution(mesh):
    return jax.shard_map(
        per_device,
        mesh=mesh,
        in_specs=(
            P("dp", None, "mp"),
            P(None, "dp", None, "mp"),
            P("dp", None, "mp"),
            P("dp"),
            P(),
            P(),
            P(("dp", "mp"), None, None, None),
            P(("dp", "mp"), None, None),
        ),
        out_specs=(
            P("dp", None, "mp"),
            P(None, "dp", None, "mp"),
            P(("dp", "mp"), None, None, None),
        ),
        check_vma=False,
    )
```

```python
import functools
import math

import jax
import jax.numpy as jnp
from jax import lax
from jax.experimental import pallas as pl
from jax.experimental.pallas import tpu as pltpu
from jax.sharding import PartitionSpec as P

DH = 128
LEAD_DP = 27
LEAD_MP = 4
SMEM = pl.BlockSpec(memory_space=pltpu.SMEM)
VMEM = pl.BlockSpec(memory_space=pltpu.VMEM)
HBM = pl.BlockSpec(memory_space=pltpu.MemorySpace.HBM)
PARAMS = pltpu.CompilerParams(vmem_limit_bytes=48 * 1024 * 1024)
INV_ROOT = 1.0 / DH**0.5
TO_EXP2 = math.log2(math.e) / DH**0.5
ACROSS = (((1,), (1,)), ((), ()))


def scale_kernel(
    chunks, lists, pages_ref, scales_ref, *refs
):
    (out0_ref, out1_ref, pages, scales, scaled0, scaled1, in_sems, out_sems, scales_sem) = refs
    rows = pages_ref.shape[0]
    groups, heads = scales_ref.shape
    step = rows // chunks
    parts = [pl.ds(c * step, step) for c in range(chunks)]
    arriving = [
        pltpu.make_async_copy(pages_ref.at[part], pages.at[part], in_sems.at[c])
        for c, part in enumerate(parts)
    ]
    outs = [(scaled0, out0_ref), (scaled1, out1_ref)]
    leaving = [
        pltpu.make_async_copy(scaled.at[:, part], out_ref.at[:, part], out_sems.at[core, c])
        for core, (scaled, out_ref) in enumerate(outs)
        for c, part in enumerate(parts)
    ]
    scales_copy = pltpu.make_async_copy(scales_ref, scales, scales_sem)
    scales_copy.start()
    for copy in arriving:
        copy.start()
    scales_copy.wait()
    factors = scales[...].astype(jnp.float32)
    factors = jnp.broadcast_to(factors[:, None, :], (groups, rows // groups, heads)).reshape(rows, heads)
    for c in range(chunks):
        arriving[c].wait()
        for core, (scaled, _) in enumerate(outs):
            for k, j in enumerate(lists[core]):
                stored = pages[c * step : (c + 1) * step, j * DH : (j + 1) * DH].astype(jnp.float32)
                factor = factors[c * step : (c + 1) * step, j : j + 1]
                scaled[k, c * step : (c + 1) * step] = (stored * factor).astype(jnp.bfloat16)
            leaving[core * chunks + c].start()
    for copy in leaving:
        copy.wait()


def dp_order(size):
    return [(LEAD_DP + k) % size for k in range(size)]


def mp_order(size):
    return [(LEAD_MP + k) % size for k in range(size)]


def index_kernel(order, send_ref, sum_ref, source_ref, send_out, sum_out, source_out):
    for k, r in enumerate(order):
        send_out[k] = send_ref[r]
        sum_out[k] = sum_ref[r]
    for i in range(source_ref.shape[0]):
        source_out[i] = source_ref[i]


def select_kernel(rows_ref, first_ref, second_ref, out_ref):
    half = first_ref.shape[0]
    for r in range(out_ref.shape[0]):
        row = rows_ref[r]
        place = lax.rem(row, half)
        out_ref[r] = jnp.where(row < half, first_ref[place], second_ref[place])


def select_chips_kernel(pages_dev, chip_ref, rows_ref, *refs):
    *arrived_refs, out_ref = refs
    chips = len(arrived_refs)
    half = chips * pages_dev
    for r in range(out_ref.shape[0]):
        row = rows_ref[r]
        core = lax.div(row, half)
        place = lax.rem(row, half)
        back = lax.rem(chip_ref[0] + chips - lax.div(place, pages_dev), chips)
        at = core * pages_dev + lax.rem(place, pages_dev)
        page = arrived_refs[0][at]
        for d in range(1, chips):
            page = jnp.where(back == d, arrived_refs[d][at], page)
        out_ref[r] = page


def pair_kernel(chip_ref, first_ref, second_ref, *out_refs):
    chips = len(out_refs)
    for d in range(chips):
        chip = lax.rem(chip_ref[0] + d, chips)
        out_refs[d][0] = first_ref[chip]
        out_refs[d][1] = second_ref[chip]


def own_kernel(
    length_ref, own_ref, q_ref, g_ref, q_rows_ref, g_rows_ref, top_ref, sum_ref, exps_ref, grad_ref
):
    resp_len = q_ref.shape[0]
    live = lax.broadcasted_iota(jnp.int32, (resp_len, DH), 0) < length_ref[0]
    key_pos = lax.broadcasted_iota(jnp.int32, (resp_len, resp_len), 0)
    row_pos = lax.broadcasted_iota(jnp.int32, (resp_len, resp_len), 1)
    for h in range(q_ref.shape[1] // DH):
        rows = slice(h * resp_len, (h + 1) * resp_len)
        q = q_ref[:, h * DH : (h + 1) * DH]
        g = g_ref[:, h * DH : (h + 1) * DH]
        g = jnp.where(live, g, jnp.zeros_like(g))
        q_rows_ref[rows] = q
        g_rows_ref[rows] = g
        scores = lax.dot_general(own_ref[0], q, ACROSS, preferred_element_type=jnp.float32)
        grad_weights = lax.dot_general(own_ref[1], g, ACROSS, preferred_element_type=jnp.float32)
        scores = jnp.where(key_pos <= row_pos, scores, -1e30)
        top = jnp.max(scores, axis=0, keepdims=True)
        exps = jnp.exp2((scores - top) * TO_EXP2)
        top_ref[:, rows] = top
        sum_ref[:, rows] = jnp.sum(exps, axis=0, keepdims=True)
        exps_ref[:, rows] = exps
        grad_ref[:, rows] = grad_weights


def gather_pages(sources_ref, arrived_ref, key_ref, value_ref):
    page_rows = arrived_ref.shape[1] // 2
    for i in range(sources_ref.shape[0]):
        slot = sources_ref[i]
        rows = slice(i * page_rows, (i + 1) * page_rows)
        key_ref[rows] = arrived_ref[slot, :page_rows]
        value_ref[rows] = arrived_ref[slot, page_rows:]


def page_grad_kernel(
    sources_ref,
    arrived_ref,
    q_ref,
    g_ref,
    top_ref,
    sum_ref,
    own_exps_ref,
    own_grad_ref,
    sent_ref,
    key_ref,
    value_ref,
):
    gather_pages(sources_ref, arrived_ref, key_ref, value_ref)
    q = q_ref[...]
    g = g_ref[...]
    scores = lax.dot_general(key_ref[...], q, ACROSS, preferred_element_type=jnp.float32)
    grad_weights = lax.dot_general(value_ref[...], g, ACROSS, preferred_element_type=jnp.float32)
    own_top = top_ref[...]
    top = jnp.maximum(jnp.max(scores, axis=0, keepdims=True), own_top)
    exps = jnp.exp2((scores - top) * TO_EXP2)
    back = jnp.exp2((own_top - top) * TO_EXP2)
    scale = 1.0 / (jnp.sum(exps, axis=0, keepdims=True) + back * sum_ref[...])
    weights = exps * scale
    weights_b = weights.astype(jnp.bfloat16)
    own_weights = (own_exps_ref[...] * (back * scale)).astype(jnp.bfloat16)
    delta = jnp.sum(weights_b.astype(jnp.float32) * grad_weights, axis=0, keepdims=True)
    delta += jnp.sum(own_weights.astype(jnp.float32) * own_grad_ref[...], axis=0, keepdims=True)
    grad_scores = (weights * (grad_weights - delta)).astype(jnp.bfloat16)
    value_grad = jnp.dot(weights_b, g, preferred_element_type=jnp.float32)
    key_grad = jnp.dot(grad_scores, q, preferred_element_type=jnp.float32) * INV_ROOT
    value_grad = value_grad.astype(jnp.bfloat16)
    key_grad = key_grad.astype(jnp.bfloat16)
    page_rows = arrived_ref.shape[1] // 2
    for i in range(sources_ref.shape[0]):
        slot = sources_ref[i]
        rows = slice(i * page_rows, (i + 1) * page_rows)
        sent_ref[slot, :page_rows] = key_grad[rows]
        sent_ref[slot, page_rows:] = value_grad[rows]


def own_grad_kernel(
    sources_ref, arrived_ref, own_ref, q_ref, g_ref, d_query_ref, d_own_ref, key_ref, value_ref
):
    resp_len = d_query_ref.shape[0]
    prompt_len = key_ref.shape[0] - resp_len
    gather_pages(sources_ref, arrived_ref, key_ref, value_ref)
    key_ref[prompt_len:] = own_ref[0]
    value_ref[prompt_len:] = own_ref[1]
    keys = key_ref[...]
    values = value_ref[...]
    keys_t = keys.astype(jnp.float32).T.astype(jnp.bfloat16)
    width = 2 * resp_len
    own_pos = lax.broadcasted_iota(jnp.int32, (resp_len, width), 0)
    row_pos = lax.broadcasted_iota(jnp.int32, (resp_len, width), 1) % resp_len
    allowed = own_pos <= row_pos
    key_grad = None
    value_grad = None
    for b in range(q_ref.shape[0] // width):
        q = q_ref[b * width : (b + 1) * width]
        g = g_ref[b * width : (b + 1) * width]
        scores = lax.dot_general(keys, q, ACROSS, preferred_element_type=jnp.float32)
        grad_weights = lax.dot_general(values, g, ACROSS, preferred_element_type=jnp.float32)
        own_scores = jnp.where(allowed, scores[prompt_len:], -1e30)
        scores = jnp.concatenate([scores[:prompt_len], own_scores], axis=0)
        exps = jnp.exp2((scores - jnp.max(scores, axis=0, keepdims=True)) * TO_EXP2)
        scale = 1.0 / jnp.sum(exps, axis=0, keepdims=True)
        weights = exps * scale
        weights_b = weights.astype(jnp.bfloat16)
        delta = jnp.sum(weights_b.astype(jnp.float32) * grad_weights, axis=0, keepdims=True)
        grad_scores = (weights * (grad_weights - delta)).astype(jnp.bfloat16)
        part = jnp.dot(weights_b[prompt_len:], g, preferred_element_type=jnp.float32)
        value_grad = part if value_grad is None else value_grad + part
        part = jnp.dot(grad_scores[prompt_len:], q, preferred_element_type=jnp.float32)
        key_grad = part if key_grad is None else key_grad + part
        d_q = jnp.dot(keys_t, grad_scores, preferred_element_type=jnp.float32) * INV_ROOT
        for k in range(2):
            head = 2 * b + k
            block = d_q[:, k * resp_len : (k + 1) * resp_len].T
            d_query_ref[:, head * DH : (head + 1) * DH] = block.astype(jnp.bfloat16)
    d_own_ref[0] = (key_grad * INV_ROOT).astype(jnp.bfloat16)
    d_own_ref[1] = value_grad.astype(jnp.bfloat16)


def sum_kernel(rows_ref, arrived_ref, out_ref, total_ref):
    pages = out_ref.shape[0]
    total_ref[...] = jnp.zeros_like(total_ref)
    for r in range(arrived_ref.shape[0]):
        row = rows_ref[r]
        total_ref[row] = total_ref[row] + arrived_ref[r].astype(jnp.float32)
    out_ref[...] = total_ref[:pages].astype(jnp.bfloat16)


def layout_kernel(order, parts_ref, out_ref, buf, sems):
    chunks = sems.shape[0]
    step = buf.shape[0] // chunks
    copies = []
    for c in range(chunks):
        part = slice(c * step, (c + 1) * step)
        for k, j in enumerate(order):
            buf[part, j * DH : (j + 1) * DH] = parts_ref[k, part].astype(jnp.float32)
        rows = pl.ds(c * step, step)
        copies.append(pltpu.make_async_copy(buf.at[rows], out_ref.at[rows], sems.at[c]))
        copies[c].start()
    for copy in copies:
        copy.wait()


def exchange(parts, axis, *groups):
    return lax.all_to_all(
        parts, axis, split_axis=0, concat_axis=0, axis_index_groups=list(groups), tiled=True
    )


def per_device(resp_q, resp_kv, d_out, lengths, fork, page_table, pool_pages, pool_scales):
    dp_size = lax.axis_size("dp")
    mp_size = lax.axis_size("mp")
    my_dp = lax.axis_index("dp")
    pool_dev, _, page_rows, _ = pool_pages.shape
    heads_kv = pool_scales.shape[-1]
    pages_prompt = page_table.shape[1]
    resp_len = resp_q.shape[1]
    q_rows_all = resp_len * (resp_q.shape[2] // DH)
    prompt_len = pages_prompt * page_rows
    total = prompt_len + resp_len
    group_rows = mp_size * pool_dev
    slot_rows = 2 * page_rows
    stored_rows = pool_dev * slot_rows
    bf16 = jnp.bfloat16

    order = dp_order(dp_size)
    heads = mp_order(mp_size)

    chunks = 4
    chips = mp_size // 2
    first_y = heads[0] // 2
    chip_order = [(first_y + k) % chips for k in range(chips)]
    lists = [[2 * y + core for y in chip_order] for core in range(2)]
    head_parts = jax.ShapeDtypeStruct((chips, stored_rows, DH), bf16)
    of_core0, of_core1 = pl.pallas_call(
        functools.partial(scale_kernel, chunks, lists),
        out_shape=(head_parts, head_parts),
        in_specs=[HBM, HBM],
        out_specs=(HBM, HBM),
        scratch_shapes=[
            pltpu.VMEM((stored_rows, heads_kv * DH), bf16),
            pltpu.VMEM((pool_dev * 2, heads_kv), bf16),
            pltpu.VMEM((chips, stored_rows, DH), bf16),
            pltpu.VMEM((chips, stored_rows, DH), bf16),
            pltpu.SemaphoreType.DMA((chunks,)),
            pltpu.SemaphoreType.DMA((2, chunks)),
            pltpu.SemaphoreType.DMA,
        ],
    )(pool_pages.reshape(stored_rows, -1), pool_scales.reshape(pool_dev * 2, heads_kv))
    from_core0 = lax.ppermute(of_core1, "mp", [(2 * y, 2 * y + 1) for y in range(chips)])
    along_y = exchange(of_core0, "mp", *lists)
    wanted = jnp.take(page_table, fork, axis=0)
    on_device = wanted // group_rows == my_dp
    send_rows = jnp.sum(jnp.where(on_device, wanted % group_rows, 0), axis=1)
    sum_rows = (send_rows + (group_rows - heads[0] * pool_dev)) % group_rows
    sum_rows = jnp.where(jnp.any(on_device, axis=1), sum_rows, group_rows)
    owner = send_rows // pool_dev
    chip = (owner // 2 + (chips - first_y)) % chips
    send_rows = owner % 2 * (group_rows // 2) + chip * pool_dev + send_rows % pool_dev
    sources = jnp.take(wanted, my_dp, axis=0) // group_rows
    sources = (sources + (dp_size - order[0])) % dp_size
    send_rows, sum_rows, sources = pl.pallas_call(
        functools.partial(index_kernel, order),
        out_shape=tuple(pltpu.MemorySpace.SMEM(v.shape, v.dtype) for v in (send_rows, sum_rows, sources)),
        in_specs=[SMEM, SMEM, SMEM],
        out_specs=(SMEM, SMEM, SMEM),
        compiler_params=PARAMS,
    )(send_rows, sum_rows, sources)

    own = resp_kv[:, 0]
    rows = jax.ShapeDtypeStruct((q_rows_all, DH), bf16)
    stat = jax.ShapeDtypeStruct((1, q_rows_all), jnp.float32)
    own_part = jax.ShapeDtypeStruct((resp_len, q_rows_all), jnp.float32)
    q_rows, g_rows, *stats = pl.pallas_call(
        own_kernel,
        out_shape=(rows, rows, stat, stat, own_part, own_part),
        in_specs=[SMEM, VMEM, VMEM, VMEM],
        out_specs=(VMEM,) * 6,
        compiler_params=PARAMS,
        cost_estimate=pl.CostEstimate(flops=10**8, bytes_accessed=2**21, transcendentals=2**17),
    )(lengths, own, resp_q[0], d_out[0])
    along_y, send_rows, q_rows, g_rows = lax.optimization_barrier((along_y, send_rows, q_rows, g_rows))
    from_core1 = lax.ppermute(along_y, "mp", [(2 * y + 1, 2 * y) for y in range(chips)])

    slots = jax.ShapeDtypeStruct((dp_size, slot_rows, DH), bf16)

    def core0(rows, own_pages, other_pages, own_heads, other_heads):
        selected = pl.pallas_call(
            select_kernel,
            out_shape=slots,
            in_specs=[SMEM, VMEM, VMEM],
            out_specs=VMEM,
            compiler_params=PARAMS,
        )(
            rows,
            own_pages.reshape(group_rows // 2, slot_rows, DH),
            other_pages.reshape(group_rows // 2, slot_rows, DH),
        )
        return exchange(selected, "dp", order)

    def core1(rows, own_pages, other_pages, own_heads, other_heads):
        chip = ((lax.axis_index("mp") // 2 + (chips - first_y)) % chips).reshape(1)
        parts = pl.pallas_call(
            pair_kernel,
            out_shape=(jax.ShapeDtypeStruct((2, stored_rows, DH), bf16),) * chips,
            in_specs=[SMEM, VMEM, VMEM],
            out_specs=(VMEM,) * chips,
            compiler_params=PARAMS,
        )(chip, other_heads, own_heads)
        moved = [parts[0]]
        for d in range(1, chips):
            pairs = [(2 * y + 1, 2 * ((y + d) % chips) + 1) for y in range(chips)]
            moved.append(lax.ppermute(parts[d], "mp", pairs))
        selected = pl.pallas_call(
            functools.partial(select_chips_kernel, pool_dev),
            out_shape=slots,
            in_specs=[SMEM, SMEM] + [VMEM] * chips,
            out_specs=VMEM,
            compiler_params=PARAMS,
        )(chip, rows, *[v.reshape(2 * pool_dev, slot_rows, DH) for v in moved])
        return exchange(selected, "dp", order)

    arrived = lax.cond(
        lax.axis_index("mp") % 2 == 0,
        core0,
        core1,
        send_rows,
        along_y,
        from_core1,
        of_core1,
        from_core0,
    )

    sent = pl.pallas_call(
        page_grad_kernel,
        out_shape=slots,
        in_specs=[SMEM] + [VMEM] * 7,
        out_specs=VMEM,
        scratch_shapes=[pltpu.VMEM((prompt_len, DH), bf16), pltpu.VMEM((prompt_len, DH), bf16)],
        compiler_params=PARAMS,
    )(sources, arrived, q_rows, g_rows, *stats)
    returned = exchange(sent, "dp", order)

    d_query, d_own = pl.pallas_call(
        own_grad_kernel,
        out_shape=(
            jax.ShapeDtypeStruct(resp_q.shape[1:], bf16),
            jax.ShapeDtypeStruct((2, resp_len, DH), bf16),
        ),
        in_specs=[SMEM] + [VMEM] * 4,
        out_specs=(VMEM, VMEM),
        scratch_shapes=[pltpu.VMEM((total, DH), bf16), pltpu.VMEM((total, DH), bf16)],
        compiler_params=PARAMS,
        cost_estimate=pl.CostEstimate(flops=2 * 10**9, bytes_accessed=2**22, transcendentals=2**20),
    )(sources, arrived, own, q_rows, g_rows)

    summed = pl.pallas_call(
        sum_kernel,
        out_shape=jax.ShapeDtypeStruct((group_rows, slot_rows, DH), bf16),
        in_specs=[SMEM, VMEM],
        out_specs=VMEM,
        scratch_shapes=[pltpu.VMEM((group_rows + 1, slot_rows, DH), jnp.float32)],
        compiler_params=PARAMS,
    )(sum_rows, returned)
    restored = exchange(summed.reshape(mp_size, stored_rows, DH), "mp", heads)
    d_pool = pl.pallas_call(
        functools.partial(layout_kernel, heads),
        out_shape=jax.ShapeDtypeStruct((stored_rows, heads_kv * DH), jnp.float32),
        in_specs=[VMEM],
        out_specs=HBM,
        scratch_shapes=[
            pltpu.VMEM((stored_rows, heads_kv * DH), jnp.float32),
            pltpu.SemaphoreType.DMA((4,)),
        ],
        compiler_params=PARAMS,
    )(restored)
    return d_query[None], d_own[:, None], d_pool.reshape(pool_pages.shape)


def solution(mesh):
    return jax.shard_map(
        per_device,
        mesh=mesh,
        in_specs=(
            P("dp", None, "mp"),
            P(None, "dp", None, "mp"),
            P("dp", None, "mp"),
            P("dp"),
            P(),
            P(),
            P(("dp", "mp"), None, None, None),
            P(("dp", "mp"), None, None),
        ),
        out_specs=(
            P("dp", None, "mp"),
            P(None, "dp", None, "mp"),
            P(("dp", "mp"), None, None, None),
        ),
        check_vma=False,
    )
```

```python
import functools
import math

import jax
import jax.numpy as jnp
from jax import lax
from jax.experimental import pallas as pl
from jax.experimental.pallas import tpu as pltpu
from jax.sharding import PartitionSpec as P

DH = 128
LEAD_DP = 27
LEAD_MP = 4
SMEM = pl.BlockSpec(memory_space=pltpu.SMEM)
VMEM = pl.BlockSpec(memory_space=pltpu.VMEM)
HBM = pl.BlockSpec(memory_space=pltpu.MemorySpace.HBM)
PARAMS = pltpu.CompilerParams(vmem_limit_bytes=48 * 1024 * 1024)
INV_ROOT = 1.0 / DH**0.5
TO_EXP2 = math.log2(math.e) / DH**0.5
ACROSS = (((1,), (1,)), ((), ()))


def scale_kernel(
    chunks, lists, pages_ref, scales_ref, *refs
):
    (out0_ref, out1_ref, pages, scales, scaled0, scaled1, in_sems, out_sems, scales_sem) = refs
    rows = pages_ref.shape[0]
    groups, heads = scales_ref.shape
    step = rows // chunks
    parts = [pl.ds(c * step, step) for c in range(chunks)]
    arriving = [
        pltpu.make_async_copy(pages_ref.at[part], pages.at[part], in_sems.at[c])
        for c, part in enumerate(parts)
    ]
    outs = [(scaled0, out0_ref), (scaled1, out1_ref)]
    leaving = [
        pltpu.make_async_copy(scaled.at[:, part], out_ref.at[:, part], out_sems.at[core, c])
        for core, (scaled, out_ref) in enumerate(outs)
        for c, part in enumerate(parts)
    ]
    scales_copy = pltpu.make_async_copy(scales_ref, scales, scales_sem)
    scales_copy.start()
    for copy in arriving:
        copy.start()
    scales_copy.wait()
    factors = scales[...].astype(jnp.float32)
    factors = jnp.broadcast_to(factors[:, None, :], (groups, rows // groups, heads)).reshape(rows, heads)
    for c in range(chunks):
        arriving[c].wait()
        for core, (scaled, _) in enumerate(outs):
            for k, j in enumerate(lists[core]):
                stored = pages[c * step : (c + 1) * step, j * DH : (j + 1) * DH].astype(jnp.float32)
                factor = factors[c * step : (c + 1) * step, j : j + 1]
                scaled[k, c * step : (c + 1) * step] = (stored * factor).astype(jnp.bfloat16)
            leaving[core * chunks + c].start()
    for copy in leaving:
        copy.wait()


def dp_order(size):
    return [(LEAD_DP + k) % size for k in range(size)]


def mp_order(size):
    return [(LEAD_MP + k) % size for k in range(size)]


def index_kernel(order, send_ref, sum_ref, source_ref, send_out, sum_out, source_out):
    for k, r in enumerate(order):
        send_out[k] = send_ref[r]
        sum_out[k] = sum_ref[r]
    for i in range(source_ref.shape[0]):
        source_out[i] = source_ref[i]


def select_kernel(rows_ref, first_ref, second_ref, out_ref):
    half = first_ref.shape[0]
    for r in range(out_ref.shape[0]):
        row = rows_ref[r]
        place = lax.rem(row, half)
        out_ref[r] = jnp.where(row < half, first_ref[place], second_ref[place])


def select_chips_kernel(pages_dev, chip_ref, rows_ref, *refs):
    *arrived_refs, out_ref, pages_ref = refs
    chips = len(arrived_refs)
    for d in range(chips):
        pages_ref[d] = arrived_refs[d][...]
    half = chips * pages_dev
    for r in range(out_ref.shape[0]):
        row = rows_ref[r]
        core = lax.div(row, half)
        place = lax.rem(row, half)
        back = lax.rem(chip_ref[0] + chips - lax.div(place, pages_dev), chips)
        out_ref[r] = pages_ref[back, core * pages_dev + lax.rem(place, pages_dev)]


def pair_kernel(chip_ref, first_ref, second_ref, *out_refs):
    chips = len(out_refs)
    for d in range(chips):
        chip = lax.rem(chip_ref[0] + d, chips)
        out_refs[d][0] = first_ref[chip]
        out_refs[d][1] = second_ref[chip]


def own_kernel(
    length_ref, own_ref, q_ref, g_ref, q_rows_ref, g_rows_ref, top_ref, sum_ref, exps_ref, grad_ref
):
    resp_len = q_ref.shape[0]
    live = lax.broadcasted_iota(jnp.int32, (resp_len, DH), 0) < length_ref[0]
    key_pos = lax.broadcasted_iota(jnp.int32, (resp_len, resp_len), 0)
    row_pos = lax.broadcasted_iota(jnp.int32, (resp_len, resp_len), 1)
    for h in range(q_ref.shape[1] // DH):
        rows = slice(h * resp_len, (h + 1) * resp_len)
        q = q_ref[:, h * DH : (h + 1) * DH]
        g = g_ref[:, h * DH : (h + 1) * DH]
        g = jnp.where(live, g, jnp.zeros_like(g))
        q_rows_ref[rows] = q
        g_rows_ref[rows] = g
        scores = lax.dot_general(own_ref[0], q, ACROSS, preferred_element_type=jnp.float32)
        grad_weights = lax.dot_general(own_ref[1], g, ACROSS, preferred_element_type=jnp.float32)
        scores = jnp.where(key_pos <= row_pos, scores, -1e30)
        top = jnp.max(scores, axis=0, keepdims=True)
        exps = jnp.exp2((scores - top) * TO_EXP2)
        top_ref[:, rows] = top
        sum_ref[:, rows] = jnp.sum(exps, axis=0, keepdims=True)
        exps_ref[:, rows] = exps
        grad_ref[:, rows] = grad_weights


def gather_pages(sources_ref, arrived_ref, key_ref, value_ref):
    page_rows = arrived_ref.shape[1] // 2
    for i in range(sources_ref.shape[0]):
        slot = sources_ref[i]
        rows = slice(i * page_rows, (i + 1) * page_rows)
        key_ref[rows] = arrived_ref[slot, :page_rows]
        value_ref[rows] = arrived_ref[slot, page_rows:]


def page_grad_kernel(
    sources_ref,
    arrived_ref,
    q_ref,
    g_ref,
    top_ref,
    sum_ref,
    own_exps_ref,
    own_grad_ref,
    sent_ref,
    key_ref,
    value_ref,
):
    gather_pages(sources_ref, arrived_ref, key_ref, value_ref)
    q = q_ref[...]
    g = g_ref[...]
    scores = lax.dot_general(key_ref[...], q, ACROSS, preferred_element_type=jnp.float32)
    grad_weights = lax.dot_general(value_ref[...], g, ACROSS, preferred_element_type=jnp.float32)
    own_top = top_ref[...]
    top = jnp.maximum(jnp.max(scores, axis=0, keepdims=True), own_top)
    exps = jnp.exp2((scores - top) * TO_EXP2)
    back = jnp.exp2((own_top - top) * TO_EXP2)
    scale = 1.0 / (jnp.sum(exps, axis=0, keepdims=True) + back * sum_ref[...])
    weights = exps * scale
    weights_b = weights.astype(jnp.bfloat16)
    own_weights = (own_exps_ref[...] * (back * scale)).astype(jnp.bfloat16)
    delta = jnp.sum(weights_b.astype(jnp.float32) * grad_weights, axis=0, keepdims=True)
    delta += jnp.sum(own_weights.astype(jnp.float32) * own_grad_ref[...], axis=0, keepdims=True)
    grad_scores = (weights * (grad_weights - delta)).astype(jnp.bfloat16)
    value_grad = jnp.dot(weights_b, g, preferred_element_type=jnp.float32)
    key_grad = jnp.dot(grad_scores, q, preferred_element_type=jnp.float32) * INV_ROOT
    value_grad = value_grad.astype(jnp.bfloat16)
    key_grad = key_grad.astype(jnp.bfloat16)
    page_rows = arrived_ref.shape[1] // 2
    for i in range(sources_ref.shape[0]):
        slot = sources_ref[i]
        rows = slice(i * page_rows, (i + 1) * page_rows)
        sent_ref[slot, :page_rows] = key_grad[rows]
        sent_ref[slot, page_rows:] = value_grad[rows]


def own_grad_kernel(
    sources_ref, arrived_ref, own_ref, q_ref, g_ref, d_query_ref, d_own_ref, key_ref, value_ref
):
    resp_len = d_query_ref.shape[0]
    prompt_len = key_ref.shape[0] - resp_len
    gather_pages(sources_ref, arrived_ref, key_ref, value_ref)
    key_ref[prompt_len:] = own_ref[0]
    value_ref[prompt_len:] = own_ref[1]
    keys = key_ref[...]
    values = value_ref[...]
    keys_t = keys.astype(jnp.float32).T.astype(jnp.bfloat16)
    width = 2 * resp_len
    own_pos = lax.broadcasted_iota(jnp.int32, (resp_len, width), 0)
    row_pos = lax.broadcasted_iota(jnp.int32, (resp_len, width), 1) % resp_len
    allowed = own_pos <= row_pos
    key_grad = None
    value_grad = None
    for b in range(q_ref.shape[0] // width):
        q = q_ref[b * width : (b + 1) * width]
        g = g_ref[b * width : (b + 1) * width]
        scores = lax.dot_general(keys, q, ACROSS, preferred_element_type=jnp.float32)
        grad_weights = lax.dot_general(values, g, ACROSS, preferred_element_type=jnp.float32)
        own_scores = jnp.where(allowed, scores[prompt_len:], -1e30)
        scores = jnp.concatenate([scores[:prompt_len], own_scores], axis=0)
        exps = jnp.exp2((scores - jnp.max(scores, axis=0, keepdims=True)) * TO_EXP2)
        scale = 1.0 / jnp.sum(exps, axis=0, keepdims=True)
        weights = exps * scale
        weights_b = weights.astype(jnp.bfloat16)
        delta = jnp.sum(weights_b.astype(jnp.float32) * grad_weights, axis=0, keepdims=True)
        grad_scores = (weights * (grad_weights - delta)).astype(jnp.bfloat16)
        part = jnp.dot(weights_b[prompt_len:], g, preferred_element_type=jnp.float32)
        value_grad = part if value_grad is None else value_grad + part
        part = jnp.dot(grad_scores[prompt_len:], q, preferred_element_type=jnp.float32)
        key_grad = part if key_grad is None else key_grad + part
        d_q = jnp.dot(keys_t, grad_scores, preferred_element_type=jnp.float32) * INV_ROOT
        for k in range(2):
            head = 2 * b + k
            block = d_q[:, k * resp_len : (k + 1) * resp_len].T
            d_query_ref[:, head * DH : (head + 1) * DH] = block.astype(jnp.bfloat16)
    d_own_ref[0] = (key_grad * INV_ROOT).astype(jnp.bfloat16)
    d_own_ref[1] = value_grad.astype(jnp.bfloat16)


def sum_kernel(rows_ref, arrived_ref, out_ref, total_ref):
    pages = out_ref.shape[0]
    total_ref[...] = jnp.zeros_like(total_ref)
    for r in range(arrived_ref.shape[0]):
        row = rows_ref[r]
        total_ref[row] = total_ref[row] + arrived_ref[r].astype(jnp.float32)
    out_ref[...] = total_ref[:pages].astype(jnp.bfloat16)


def layout_kernel(order, parts_ref, out_ref, buf, sems):
    chunks = sems.shape[0]
    step = buf.shape[0] // chunks
    copies = []
    for c in range(chunks):
        part = slice(c * step, (c + 1) * step)
        for k, j in enumerate(order):
            buf[part, j * DH : (j + 1) * DH] = parts_ref[k, part].astype(jnp.float32)
        rows = pl.ds(c * step, step)
        copies.append(pltpu.make_async_copy(buf.at[rows], out_ref.at[rows], sems.at[c]))
        copies[c].start()
    for copy in copies:
        copy.wait()


def exchange(parts, axis, *groups):
    return lax.all_to_all(
        parts, axis, split_axis=0, concat_axis=0, axis_index_groups=list(groups), tiled=True
    )


def per_device(resp_q, resp_kv, d_out, lengths, fork, page_table, pool_pages, pool_scales):
    dp_size = lax.axis_size("dp")
    mp_size = lax.axis_size("mp")
    my_dp = lax.axis_index("dp")
    pool_dev, _, page_rows, _ = pool_pages.shape
    heads_kv = pool_scales.shape[-1]
    pages_prompt = page_table.shape[1]
    resp_len = resp_q.shape[1]
    q_rows_all = resp_len * (resp_q.shape[2] // DH)
    prompt_len = pages_prompt * page_rows
    total = prompt_len + resp_len
    group_rows = mp_size * pool_dev
    slot_rows = 2 * page_rows
    stored_rows = pool_dev * slot_rows
    bf16 = jnp.bfloat16

    order = dp_order(dp_size)
    heads = mp_order(mp_size)

    chunks = 4
    chips = mp_size // 2
    first_y = heads[0] // 2
    chip_order = [(first_y + k) % chips for k in range(chips)]
    lists = [[2 * y + core for y in chip_order] for core in range(2)]
    head_parts = jax.ShapeDtypeStruct((chips, stored_rows, DH), bf16)
    of_core0, of_core1 = pl.pallas_call(
        functools.partial(scale_kernel, chunks, lists),
        out_shape=(head_parts, head_parts),
        in_specs=[HBM, HBM],
        out_specs=(HBM, HBM),
        scratch_shapes=[
            pltpu.VMEM((stored_rows, heads_kv * DH), bf16),
            pltpu.VMEM((pool_dev * 2, heads_kv), bf16),
            pltpu.VMEM((chips, stored_rows, DH), bf16),
            pltpu.VMEM((chips, stored_rows, DH), bf16),
            pltpu.SemaphoreType.DMA((chunks,)),
            pltpu.SemaphoreType.DMA((2, chunks)),
            pltpu.SemaphoreType.DMA,
        ],
    )(pool_pages.reshape(stored_rows, -1), pool_scales.reshape(pool_dev * 2, heads_kv))
    from_core0 = lax.ppermute(of_core1, "mp", [(2 * y, 2 * y + 1) for y in range(chips)])
    along_y = exchange(of_core0, "mp", *lists)
    wanted = jnp.take(page_table, fork, axis=0)
    on_device = wanted // group_rows == my_dp
    send_rows = jnp.sum(jnp.where(on_device, wanted % group_rows, 0), axis=1)
    sum_rows = (send_rows + (group_rows - heads[0] * pool_dev)) % group_rows
    sum_rows = jnp.where(jnp.any(on_device, axis=1), sum_rows, group_rows)
    owner = send_rows // pool_dev
    chip = (owner // 2 + (chips - first_y)) % chips
    send_rows = owner % 2 * (group_rows // 2) + chip * pool_dev + send_rows % pool_dev
    sources = jnp.take(wanted, my_dp, axis=0) // group_rows
    sources = (sources + (dp_size - order[0])) % dp_size
    send_rows, sum_rows, sources = pl.pallas_call(
        functools.partial(index_kernel, order),
        out_shape=tuple(pltpu.MemorySpace.SMEM(v.shape, v.dtype) for v in (send_rows, sum_rows, sources)),
        in_specs=[SMEM, SMEM, SMEM],
        out_specs=(SMEM, SMEM, SMEM),
        compiler_params=PARAMS,
    )(send_rows, sum_rows, sources)

    own = resp_kv[:, 0]
    rows = jax.ShapeDtypeStruct((q_rows_all, DH), bf16)
    stat = jax.ShapeDtypeStruct((1, q_rows_all), jnp.float32)
    own_part = jax.ShapeDtypeStruct((resp_len, q_rows_all), jnp.float32)
    q_rows, g_rows, *stats = pl.pallas_call(
        own_kernel,
        out_shape=(rows, rows, stat, stat, own_part, own_part),
        in_specs=[SMEM, VMEM, VMEM, VMEM],
        out_specs=(VMEM,) * 6,
        compiler_params=PARAMS,
        cost_estimate=pl.CostEstimate(flops=10**8, bytes_accessed=2**21, transcendentals=2**17),
    )(lengths, own, resp_q[0], d_out[0])
    along_y, send_rows = lax.optimization_barrier((along_y, send_rows))
    from_core1 = lax.ppermute(along_y, "mp", [(2 * y + 1, 2 * y) for y in range(chips)])
    from_core1, q_rows, g_rows = lax.optimization_barrier((from_core1, q_rows, g_rows))

    slots = jax.ShapeDtypeStruct((dp_size, slot_rows, DH), bf16)

    def core0(rows, own_pages, other_pages, own_heads, other_heads):
        selected = pl.pallas_call(
            select_kernel,
            out_shape=slots,
            in_specs=[SMEM, VMEM, VMEM],
            out_specs=VMEM,
            compiler_params=PARAMS,
        )(
            rows,
            own_pages.reshape(group_rows // 2, slot_rows, DH),
            other_pages.reshape(group_rows // 2, slot_rows, DH),
        )
        return exchange(selected, "dp", order)

    def core1(rows, own_pages, other_pages, own_heads, other_heads):
        chip = ((lax.axis_index("mp") // 2 + (chips - first_y)) % chips).reshape(1)
        parts = pl.pallas_call(
            pair_kernel,
            out_shape=(jax.ShapeDtypeStruct((2, stored_rows, DH), bf16),) * chips,
            in_specs=[SMEM, VMEM, VMEM],
            out_specs=(VMEM,) * chips,
            compiler_params=PARAMS,
        )(chip, other_heads, own_heads)
        moved = [parts[0]]
        for d in range(1, chips):
            pairs = [(2 * y + 1, 2 * ((y + d) % chips) + 1) for y in range(chips)]
            moved.append(lax.ppermute(parts[d], "mp", pairs))
        selected = pl.pallas_call(
            functools.partial(select_chips_kernel, pool_dev),
            out_shape=slots,
            in_specs=[SMEM, SMEM] + [VMEM] * chips,
            out_specs=VMEM,
            scratch_shapes=[pltpu.VMEM((chips, 2 * pool_dev, slot_rows, DH), bf16)],
            compiler_params=PARAMS,
        )(chip, rows, *[v.reshape(2 * pool_dev, slot_rows, DH) for v in moved])
        return exchange(selected, "dp", order)

    arrived = lax.cond(
        lax.axis_index("mp") % 2 == 0,
        core0,
        core1,
        send_rows,
        along_y,
        from_core1,
        of_core1,
        from_core0,
    )

    sent = pl.pallas_call(
        page_grad_kernel,
        out_shape=slots,
        in_specs=[SMEM] + [VMEM] * 7,
        out_specs=VMEM,
        scratch_shapes=[pltpu.VMEM((prompt_len, DH), bf16), pltpu.VMEM((prompt_len, DH), bf16)],
        compiler_params=PARAMS,
    )(sources, arrived, q_rows, g_rows, *stats)
    returned = exchange(sent, "dp", order)

    d_query, d_own = pl.pallas_call(
        own_grad_kernel,
        out_shape=(
            jax.ShapeDtypeStruct(resp_q.shape[1:], bf16),
            jax.ShapeDtypeStruct((2, resp_len, DH), bf16),
        ),
        in_specs=[SMEM] + [VMEM] * 4,
        out_specs=(VMEM, VMEM),
        scratch_shapes=[pltpu.VMEM((total, DH), bf16), pltpu.VMEM((total, DH), bf16)],
        compiler_params=PARAMS,
        cost_estimate=pl.CostEstimate(flops=2 * 10**9, bytes_accessed=2**22, transcendentals=2**20),
    )(sources, arrived, own, q_rows, g_rows)

    summed = pl.pallas_call(
        sum_kernel,
        out_shape=jax.ShapeDtypeStruct((group_rows, slot_rows, DH), bf16),
        in_specs=[SMEM, VMEM],
        out_specs=VMEM,
        scratch_shapes=[pltpu.VMEM((group_rows + 1, slot_rows, DH), jnp.float32)],
        compiler_params=PARAMS,
    )(sum_rows, returned)
    restored = exchange(summed.reshape(mp_size, stored_rows, DH), "mp", heads)
    d_pool = pl.pallas_call(
        functools.partial(layout_kernel, heads),
        out_shape=jax.ShapeDtypeStruct((stored_rows, heads_kv * DH), jnp.float32),
        in_specs=[VMEM],
        out_specs=HBM,
        scratch_shapes=[
            pltpu.VMEM((stored_rows, heads_kv * DH), jnp.float32),
            pltpu.SemaphoreType.DMA((4,)),
        ],
        compiler_params=PARAMS,
    )(restored)
    return d_query[None], d_own[:, None], d_pool.reshape(pool_pages.shape)


def solution(mesh):
    return jax.shard_map(
        per_device,
        mesh=mesh,
        in_specs=(
            P("dp", None, "mp"),
            P(None, "dp", None, "mp"),
            P("dp", None, "mp"),
            P("dp"),
            P(),
            P(),
            P(("dp", "mp"), None, None, None),
            P(("dp", "mp"), None, None),
        ),
        out_specs=(
            P("dp", None, "mp"),
            P(None, "dp", None, "mp"),
            P(("dp", "mp"), None, None, None),
        ),
        check_vma=False,
    )
```
